32 devices in a mesh: lat: 16 (over z, x, core), lon: 2 (over y).
Axes of the slice: x: 2, y: 2, z: 4, core: 2. Of those that a mesh axis runs over, the one named last changes fastest.
Arguments:
- grid_input: bfloat16 [352, 1440, 256], P('lat', 'lon'), may hold values from -1.5 to 1.5
- cotangent: bfloat16 [352, 1440, 256], P('lat', 'lon'), may hold values from -6 to 6
- mixing: bfloat16 [192, 256, 256], P('lat', 'lon'), may hold values from -0.375 to 0.375
Outputs:
- input_grad: bfloat16 [352, 1440, 256], P('lat', 'lon')
- weight_grad: float32 [192, 256, 256], P('lat', 'lon')
The draws below stay inside these ranges and needn't reach their ends.
All inputs are finite; a program needn't handle non-finite values.
Results may differ from the reference program's by a relative error of at most 0.0083.
Values may be sent and summed in bfloat16 or wider, within the bound.
A program may use at most 128 MiB of HBM per device.

```python
import math
import jax
import jax.numpy as jnp
from jax import lax

C = 256
NLON = 1440
LAT_DEV = 22
ORD_DEV = 12
NLAT = 352
M = 192
L = 192
N_LAT = 16


def shard_levels(key, extent, shards, low, top_value):
    level = 1.0
    for position, shards_of in shards:
        heights = jax.random.uniform(jax.random.fold_in(jax.random.fold_in(key, 6), position), (shards_of,), jnp.float32, low / len(shards), top_value / len(shards))
        level = level * jnp.repeat(jnp.exp(heights), extent[position] // shards_of).reshape((-1,) + (1,) * (len(extent) - 1 - position))
    return level


def noise(stream_key, dims, spread, reach, cuts=(), kind=jnp.bfloat16):
    values = jax.random.normal(stream_key, dims, jnp.float32) * spread
    if len(cuts) > 0:
        values = shard_levels(stream_key, dims, cuts, -0.22, 0.18) * values
    return jnp.clip(values, min=-reach, max=reach).astype(kind)


def setup_inputs(seed: int = 0) -> dict:
    splits = jax.random.split(jax.random.key(seed), 4)
    return {
        "grid_input": noise(splits[0], (NLAT, NLON, C), 0.25, 1.5, ((0, 16), (1, 2))),
        "cotangent": noise(splits[1], (NLAT, NLON, C), 1.0, 6.0, ((0, 16), (1, 2))),
        "mixing": noise(splits[2], (L, C, C), C ** -0.5, 0.375, ((0, 16), (1, 2))),
    }


def quadrature(count_lat):
    colatitude = (jnp.arange(count_lat, dtype=jnp.float32) + 0.5) * (math.pi / count_lat)
    return math.pi / count_lat * jnp.sin(colatitude)

def degree_block(degrees):
    for width in (16, 8, 4, 2):
        if degrees % width == 0:
            return width
    return 1

def legendre_table(order_ids, count_lat, degrees, order_cap):
    colatitude = (jnp.arange(count_lat, dtype=jnp.float32) + 0.5) * (math.pi / count_lat)
    cosine = jnp.cos(colatitude)[None, :]
    sine_row = jnp.sin(colatitude)[None, :]
    order_value = order_ids.astype(jnp.float32)[:, None]
    counter = jnp.arange(1, order_cap + 1, dtype=jnp.float32)[None, :]
    log_terms = jnp.where(counter <= order_value, jnp.log1p(0.5 / counter), 0.0)
    log_start = 0.5 * math.log(0.5) + 0.5 * lax.optimization_barrier(jnp.sum(log_terms, axis=1, keepdims=True)) + order_value * jnp.log(sine_row)
    zero_state = jnp.zeros((order_ids.shape[0], count_lat), jnp.float32)
    width = degree_block(degrees)

    def advance(carried, degree):
        previous, earlier, scale_log = carried
        growth = jnp.sqrt((4.0 * degree * degree - 1.0) / jnp.maximum(degree * degree - order_value * order_value, 1.0))
        shrink = jnp.sqrt(jnp.maximum((degree - 1.0) * (degree - 1.0) - order_value * order_value, 0.0) / jnp.maximum(4.0 * (degree - 1.0) * (degree - 1.0) - 1.0, 1.0))
        recurred = growth * (cosine * previous - shrink * earlier)
        first_step = cosine * jnp.sqrt(2.0 * order_value + 3.0) * previous
        current = jnp.where(degree == order_value, 1.0, jnp.where(degree == order_value + 1.0, first_step, jnp.where(degree > order_value, recurred, 0.0)))
        oversized = jnp.abs(current) > 10000000000.0
        factor = jnp.where(oversized, 1e-10, 1.0)
        scale_log = scale_log + jnp.where(oversized, math.log(10000000000.0), 0.0)
        current = current * factor
        stored = (current * jnp.exp(scale_log)).astype(jnp.bfloat16)
        return ((current, previous * factor, scale_log), stored)

    def advance_block(carried, block_start):
        stored_list = []
        for step in range(width):
            carried, stored = advance(carried, block_start + float(step))
            stored_list.append(stored)
        return (carried, jnp.stack(stored_list, axis=0))
    initial = (zero_state, zero_state, log_start + zero_state)
    starts = jnp.arange(degrees // width, dtype=jnp.float32) * float(width)
    _, blocks = lax.scan(advance_block, initial, starts)
    return blocks.reshape(degrees, order_ids.shape[0], count_lat)

def fourier_tables(order_ids, count_lon):
    points = jnp.arange(count_lon, dtype=jnp.int32)
    phase_index = points[:, None] * order_ids[None, :] % count_lon
    angles = phase_index.astype(jnp.float32) * (2.0 * math.pi / count_lon)
    forward = jnp.stack([jnp.cos(angles), -jnp.sin(angles)], axis=2).reshape(count_lon, 2 * order_ids.shape[0])
    factor = jnp.where(order_ids == 0, 1.0, 2.0).astype(jnp.float32) / count_lon
    backward = forward * jnp.repeat(factor, 2)[None, :]
    return (forward.astype(jnp.bfloat16), backward.astype(jnp.bfloat16))

def reference(grid_input, cotangent, mixing):
    order_ids = jnp.arange(M, dtype=jnp.int32)
    forward, backward = fourier_tables(order_ids, NLON)
    forward_f = forward.astype(jnp.float32)
    backward_f = backward.astype(jnp.float32)
    weights = quadrature(NLAT)

    def analyse_rows(row_block):
        block_x, block_g, block_w = row_block
        spec_x = jnp.einsum('jkc,kq->jqc', block_x.astype(jnp.float32), forward_f) * block_w[:, None, None]
        spec_g = jnp.einsum('jkc,kq->jqc', block_g.astype(jnp.float32), backward_f)
        return (spec_x.astype(jnp.bfloat16), spec_g.astype(jnp.bfloat16))
    spectra_x, spectra_g = lax.map(analyse_rows, (grid_input.reshape(N_LAT, LAT_DEV, NLON, C), cotangent.reshape(N_LAT, LAT_DEV, NLON, C), weights.reshape(N_LAT, LAT_DEV)))
    spectra_x = spectra_x.reshape(NLAT, 2 * M, C)
    spectra_g = spectra_g.reshape(NLAT, 2 * M, C)
    mixing_f = mixing.astype(jnp.float32)

    def per_block(grad_total, block_index):
        first_order = block_index * ORD_DEV
        legendre = legendre_table(first_order + jnp.arange(ORD_DEV, dtype=jnp.int32), NLAT, L, M).astype(jnp.float32)
        piece_x = lax.dynamic_slice_in_dim(spectra_x, 2 * first_order, 2 * ORD_DEV, 1).astype(jnp.float32).reshape(NLAT, ORD_DEV, 2, C)
        piece_g = lax.dynamic_slice_in_dim(spectra_g, 2 * first_order, 2 * ORD_DEV, 1).astype(jnp.float32).reshape(NLAT, ORD_DEV, 2, C)
        coefficients = lax.optimization_barrier(jnp.einsum('lmj,jmrc->mlrc', legendre, piece_x).astype(jnp.bfloat16)).astype(jnp.float32)
        adjoint = lax.optimization_barrier(jnp.einsum('lmj,jmrc->mlrc', legendre, piece_g).astype(jnp.bfloat16)).astype(jnp.float32)
        mixed = lax.optimization_barrier(jnp.einsum('mlrc,lic->mlri', adjoint, mixing_f).astype(jnp.bfloat16)).astype(jnp.float32)
        grad_total = grad_total + jnp.einsum('mlri,mlrc->lic', coefficients, adjoint)
        back_rows = jnp.einsum('lmj,mlrc->jmrc', legendre, mixed) * weights[:, None, None, None]
        return (grad_total, back_rows.astype(jnp.bfloat16).reshape(NLAT, 2 * ORD_DEV, C))
    weight_grad, pieces = lax.scan(per_block, jnp.zeros((L, C, C), jnp.float32), jnp.arange(N_LAT, dtype=jnp.int32))
    spectral_back = jnp.transpose(pieces, (1, 0, 2, 3)).reshape(NLAT, 2 * M, C)

    def synthesise_rows(row_block):
        block_h, block_g = row_block
        grid_back = jnp.einsum('jqc,kq->jkc', block_h.astype(jnp.float32), forward_f)
        grid_back = lax.optimization_barrier(grid_back.astype(jnp.bfloat16)).astype(jnp.float32)
        return (block_g.astype(jnp.float32) + grid_back).astype(jnp.bfloat16)
    input_grad = lax.map(synthesise_rows, (spectral_back.reshape(N_LAT, LAT_DEV, 2 * M, C), cotangent.reshape(N_LAT, LAT_DEV, NLON, C)))
    return (input_grad.reshape(NLAT, NLON, C), weight_grad)
```

```python
import math

import jax
import jax.numpy as jnp
from jax import lax
from jax.experimental import pallas as pl
from jax.experimental.pallas import tpu as pltpu
from jax.sharding import PartitionSpec as P


def quadrature(count_lat):
    colatitude = (jnp.arange(count_lat, dtype=jnp.float32) + 0.5) * (math.pi / count_lat)
    return math.pi / count_lat * jnp.sin(colatitude)


BLOCK = 16


def legendre_kernel(order_ref, cosine_ref, start_ref, out_ref, rows_ref):
    order = order_ref[...]
    cosine = cosine_ref[...]
    first_scale = jnp.sqrt(2.0 * order + 3.0)

    def advance(degree, carried):
        previous, earlier, scale_log = carried
        growth = jnp.sqrt(
            (4.0 * degree * degree - 1.0) / jnp.maximum(degree * degree - order * order, 1.0)
        )
        below = (degree - 1.0) * (degree - 1.0)
        shrink = jnp.sqrt(
            jnp.maximum(below - order * order, 0.0) / jnp.maximum(4.0 * below - 1.0, 1.0)
        )
        growth = jnp.where(degree == order + 1.0, first_scale, growth)
        growth = jnp.where(degree > order, growth, 0.0)
        current = growth * (cosine * previous - shrink * earlier)
        current = jnp.where(degree == order, 1.0, current)
        oversized = jnp.abs(current) > 10000000000.0
        factor = jnp.where(oversized, 1e-10, 1.0)
        scale_log = scale_log + jnp.where(oversized, math.log(10000000000.0), 0.0)
        current = current * factor
        return (current, previous * factor, scale_log), current * jnp.exp(scale_log)

    def block(index, carried):
        base = index * BLOCK
        for step in range(BLOCK):
            degree = (base + step).astype(jnp.float32)
            carried, value = advance(degree, carried)
            rows_ref[:, step, :] = value
        out_ref[:, pl.ds(pl.multiple_of(base, BLOCK), BLOCK), :] = rows_ref[...].astype(
            jnp.bfloat16
        )
        return carried

    zero = jnp.zeros(start_ref.shape, jnp.float32)
    lax.fori_loop(0, out_ref.shape[1] // BLOCK, block, (zero, zero, start_ref[...]))


def legendre_table(order_ids, count_lat, degrees, order_cap):
    colatitude = (jnp.arange(count_lat, dtype=jnp.float32) + 0.5) * (math.pi / count_lat)
    cosine = jnp.cos(colatitude)[None, :]
    sine_row = jnp.sin(colatitude)[None, :]
    order_value = order_ids.astype(jnp.float32)[:, None]
    counter = jnp.arange(1, order_cap + 1, dtype=jnp.float32)[None, :]
    log_terms = jnp.where(counter <= order_value, jnp.log1p(0.5 / counter), 0.0)
    log_start = (
        0.5 * math.log(0.5)
        + 0.5 * jnp.sum(log_terms, axis=1, keepdims=True)
        + order_value * jnp.log(sine_row)
    )
    orders = order_ids.shape[0]
    return pl.pallas_call(
        legendre_kernel,
        out_shape=jax.ShapeDtypeStruct((orders, degrees, count_lat), jnp.bfloat16),
        in_specs=[pl.BlockSpec(memory_space=pltpu.VMEM)] * 3,
        out_specs=pl.BlockSpec(memory_space=pltpu.VMEM),
        scratch_shapes=[pltpu.VMEM((orders, BLOCK, count_lat), jnp.float32)],
        compiler_params=pltpu.CompilerParams(vmem_limit_bytes=48 * 1024 * 1024),
    )(order_value, cosine, log_start)


def fourier_tables(order_ids, first, points_held, count_lon):
    points = first + jnp.arange(points_held, dtype=jnp.int32)
    phase_index = points[:, None] * order_ids[None, :] % count_lon
    angles = phase_index.astype(jnp.float32) * (2.0 * math.pi / count_lon)
    forward = jnp.stack([jnp.cos(angles), -jnp.sin(angles)], axis=2).reshape(
        points_held, 2 * order_ids.shape[0]
    )
    factor = jnp.where(order_ids == 0, 1.0, 2.0).astype(jnp.float32) / count_lon
    backward = forward * jnp.repeat(factor, 2)[None, :]
    return (forward.astype(jnp.bfloat16), backward.astype(jnp.bfloat16))


def swap(block, axis):
    return lax.all_to_all(block, axis, split_axis=0, concat_axis=0, tiled=True)


def partial_spectrum(field, table, scale, lon_count):
    rows, _, channels = field.shape
    part = jnp.einsum("jkc,kq->jqc", field, table, preferred_element_type=jnp.float32)
    if scale is not None:
        part = part * scale[:, None, None]
    part = part.astype(jnp.bfloat16).reshape(rows, -1, lon_count, channels // lon_count)
    return part.transpose(2, 1, 0, 3)


def local(grid_input, cotangent, mixing):
    lat_count = lax.axis_size("lat")
    lon_count = lax.axis_size("lon")
    lat_rows, lon_rows, channels = grid_input.shape
    count_lat = lat_rows * lat_count
    count_lon = lon_rows * lon_count
    per_dev = mixing.shape[0]
    order_total = per_dev * lat_count
    block_ch = channels // lon_count
    lat_pos = lax.axis_index("lat")
    lon_pos = lax.axis_index("lon")
    slot_ids = jnp.arange(order_total, dtype=jnp.int32)
    forward, backward = fourier_tables(slot_ids, lon_pos * lon_rows, lon_rows, count_lon)
    weights = quadrature(count_lat)
    own_weights = lax.dynamic_slice_in_dim(weights, lat_pos * lat_rows, lat_rows)
    own_orders = lat_pos * per_dev + jnp.arange(per_dev, dtype=jnp.int32)
    legendre = legendre_table(own_orders, count_lat, order_total, order_total)

    def analyse(part):
        full = swap(part, "lon").astype(jnp.float32).sum(0).astype(jnp.bfloat16)
        full = full.reshape(lat_count, per_dev, 2, lat_rows, block_ch)
        rows = swap(full, "lat")
        rows = rows.transpose(1, 0, 3, 2, 4).reshape(per_dev, count_lat, 2 * block_ch)
        out = jnp.einsum("mlj,mjc->mlc", legendre, rows, preferred_element_type=jnp.float32)
        out = out.astype(jnp.bfloat16).reshape(per_dev, lat_count, per_dev, 2, block_ch)
        out = swap(out.transpose(1, 2, 0, 3, 4), "lat")
        return out.transpose(1, 0, 2, 3, 4).reshape(per_dev, 2 * order_total, block_ch)

    adjoint = analyse(partial_spectrum(cotangent, backward, None, lon_count))
    full_adjoint = lax.all_gather(adjoint, "lon", axis=0)
    full_adjoint = full_adjoint.transpose(1, 2, 0, 3).reshape(per_dev, 2 * order_total, channels)
    mixed = jnp.einsum(
        "lqc,lic->lqi", full_adjoint, mixing, preferred_element_type=jnp.float32
    ).astype(jnp.bfloat16)
    mixed = mixed.reshape(per_dev, lat_count, per_dev, 2, block_ch).transpose(1, 0, 2, 3, 4)
    mixed = swap(mixed, "lat").transpose(2, 0, 1, 3, 4)
    mixed = mixed.reshape(per_dev, order_total, 2 * block_ch)
    back = jnp.einsum("mlj,mlc->mjc", legendre, mixed, preferred_element_type=jnp.float32)
    back = (back * weights[None, :, None]).astype(jnp.bfloat16)
    back = back.reshape(per_dev, lat_count, lat_rows, 2, block_ch).transpose(1, 2, 0, 3, 4)
    back = swap(back, "lat").transpose(1, 0, 2, 3, 4).reshape(lat_rows, 2 * order_total, block_ch)
    back = lax.all_gather(back, "lon", axis=0)
    back = back.transpose(1, 2, 0, 3).reshape(lat_rows, 2 * order_total, channels)
    grid_back = jnp.einsum("jqc,kq->jkc", back, forward, preferred_element_type=jnp.float32)
    grid_back = grid_back.astype(jnp.bfloat16).astype(jnp.float32)
    input_grad = (cotangent.astype(jnp.float32) + grid_back).astype(jnp.bfloat16)
    coefficients = analyse(partial_spectrum(grid_input, forward, own_weights, lon_count))
    weight_grad = jnp.einsum(
        "lqi,lqc->lic", coefficients, full_adjoint, preferred_element_type=jnp.float32
    )
    return (input_grad, weight_grad)


def solution(mesh):
    in_specs = (P("lat", "lon", None), P("lat", "lon", None), P("lat", "lon", None))
    out_specs = (P("lat", "lon", None), P("lat", "lon", None))
    return jax.shard_map(local, mesh=mesh, in_specs=in_specs, out_specs=out_specs, check_vma=False)
```

```python
import functools
import math

import jax
import jax.numpy as jnp
from jax import lax
from jax.experimental import pallas as pl
from jax.experimental.pallas import tpu as pltpu
from jax.sharding import PartitionSpec as P


def quadrature(count_lat):
    colatitude = (jnp.arange(count_lat, dtype=jnp.float32) + 0.5) * (math.pi / count_lat)
    return math.pi / count_lat * jnp.sin(colatitude)


BLOCK = 16


def legendre_kernel(order_ref, cosine_ref, start_ref, out_ref, rows_ref):
    order = order_ref[...]
    cosine = cosine_ref[...]
    first_scale = jnp.sqrt(2.0 * order + 3.0)

    def advance(degree, carried):
        previous, earlier, scale_log = carried
        growth = jnp.sqrt(
            (4.0 * degree * degree - 1.0) / jnp.maximum(degree * degree - order * order, 1.0)
        )
        below = (degree - 1.0) * (degree - 1.0)
        shrink = jnp.sqrt(
            jnp.maximum(below - order * order, 0.0) / jnp.maximum(4.0 * below - 1.0, 1.0)
        )
        growth = jnp.where(degree == order + 1.0, first_scale, growth)
        growth = jnp.where(degree > order, growth, 0.0)
        current = growth * (cosine * previous - shrink * earlier)
        current = jnp.where(degree == order, 1.0, current)
        oversized = jnp.abs(current) > 10000000000.0
        factor = jnp.where(oversized, 1e-10, 1.0)
        scale_log = scale_log + jnp.where(oversized, math.log(10000000000.0), 0.0)
        current = current * factor
        return (current, previous * factor, scale_log), current * jnp.exp(scale_log)

    def block(index, carried):
        base = index * BLOCK
        for step in range(BLOCK):
            degree = (base + step).astype(jnp.float32)
            carried, value = advance(degree, carried)
            rows_ref[:, step, :] = value
        out_ref[:, pl.ds(pl.multiple_of(base, BLOCK), BLOCK), :] = rows_ref[...].astype(
            jnp.bfloat16
        )
        return carried

    zero = jnp.zeros(start_ref.shape, jnp.float32)
    lax.fori_loop(0, out_ref.shape[1] // BLOCK, block, (zero, zero, start_ref[...]))


def legendre_table(order_ids, count_lat, degrees, order_cap):
    colatitude = (jnp.arange(count_lat, dtype=jnp.float32) + 0.5) * (math.pi / count_lat)
    cosine = jnp.cos(colatitude)[None, :]
    sine_row = jnp.sin(colatitude)[None, :]
    order_value = order_ids.astype(jnp.float32)[:, None]
    counter = jnp.arange(1, order_cap + 1, dtype=jnp.float32)[None, :]
    log_terms = jnp.where(counter <= order_value, jnp.log1p(0.5 / counter), 0.0)
    log_start = (
        0.5 * math.log(0.5)
        + 0.5 * jnp.sum(log_terms, axis=1, keepdims=True)
        + order_value * jnp.log(sine_row)
    )
    orders = order_ids.shape[0]
    return pl.pallas_call(
        legendre_kernel,
        out_shape=jax.ShapeDtypeStruct((orders, degrees, count_lat), jnp.bfloat16),
        in_specs=[pl.BlockSpec(memory_space=pltpu.VMEM)] * 3,
        out_specs=pl.BlockSpec(memory_space=pltpu.VMEM),
        scratch_shapes=[pltpu.VMEM((orders, BLOCK, count_lat), jnp.float32)],
        compiler_params=pltpu.CompilerParams(vmem_limit_bytes=48 * 1024 * 1024),
    )(order_value, cosine, log_start)


def fourier_tables(order_ids, first, points_held, count_lon):
    points = first + jnp.arange(points_held, dtype=jnp.int32)
    phase_index = points[:, None] * order_ids[None, :] % count_lon
    angles = phase_index.astype(jnp.float32) * (2.0 * math.pi / count_lon)
    forward = jnp.stack([jnp.cos(angles), -jnp.sin(angles)], axis=2).reshape(
        points_held, 2 * order_ids.shape[0]
    )
    factor = jnp.where(order_ids == 0, 1.0, 2.0).astype(jnp.float32) / count_lon
    backward = forward * jnp.repeat(factor, 2)[None, :]
    return (forward.astype(jnp.bfloat16), backward.astype(jnp.bfloat16))


MESH = pl.DeviceIdType.MESH
VMEM = pl.BlockSpec(memory_space=pltpu.VMEM)
SMEM = pl.BlockSpec(memory_space=pltpu.SMEM)
ANY = pl.BlockSpec(memory_space=pl.ANY)


def limits(**more):
    return pltpu.CompilerParams(vmem_limit_bytes=48 * 1024 * 1024, **more)


def peer(axis, count, offset):
    return lax.rem(lax.axis_index(axis) + offset + count, count)


def swap_copy(source, target, sems, axis, count, offset):
    there = peer(axis, count, offset)
    return pltpu.make_async_remote_copy(
        src_ref=source.at[there],
        dst_ref=target.at[lax.axis_index(axis)],
        send_sem=sems.at[0, offset],
        recv_sem=sems.at[1, offset],
        device_id={axis: there},
        device_id_type=MESH,
    )


def spread_copy(target, slot, sems, offset, step, lon_count):
    here = lax.axis_index("lon")
    return pltpu.make_async_remote_copy(
        src_ref=target.at[here, slot],
        dst_ref=target.at[here, slot],
        send_sem=sems.at[0, offset, step],
        recv_sem=sems.at[1, offset, step],
        device_id={"lon": peer("lon", lon_count, offset)},
        device_id_type=MESH,
    )


def exchange_kernel(jobs, counts, *refs):
    total = len(jobs)
    sources, targets, sems = refs[:total], refs[total : 2 * total], refs[2 * total :]
    lat_count, lon_count = counts["lat"], counts["lon"]
    axes = [axis for axis in ("lon", "lat") if axis in jobs or "spread" in jobs]

    barrier = pltpu.get_barrier_semaphore()
    expected = 0
    for axis in axes:

        def greet(offset, carried, axis=axis):
            there = peer(axis, counts[axis], offset)
            pl.semaphore_signal(barrier, inc=1, device_id={axis: there}, device_id_type=MESH)
            return carried

        lax.fori_loop(1, counts[axis], greet, 0)
        expected += counts[axis] - 1
    pl.semaphore_wait(barrier, expected)

    place = 0
    plans = []
    for kind, source, target in zip(jobs, sources, targets):
        axis = "lat" if kind == "spread" else kind
        landing = target.at[lax.axis_index("lon")] if kind == "spread" else target
        own = pltpu.make_async_copy(
            source.at[lax.axis_index(axis)], landing.at[lax.axis_index(axis)], sems[place]
        )
        plans.append((kind, axis, source, landing, target, own, sems[place + 1], sems[place + 2]))
        place += 3
    for kind, axis, source, landing, target, own, first, second in plans:

        def start(offset, carried, plan=(source, landing, first, axis, counts[axis])):
            swap_copy(*plan, offset).start()
            return carried

        lax.fori_loop(1, counts[axis], start, 0)
        own.start()
    for kind, axis, source, landing, target, own, first, second in plans:
        own.wait()
        if kind == "spread":
            for ahead in range(1, lon_count):
                spread_copy(target, peer("lat", lat_count, 0), second, ahead, 0, lon_count).start()

        def arrive(offset, carried, plan=(source, landing, first, axis, counts[axis])):
            swap_copy(*plan, offset).wait_recv()
            return carried

        def arrive_and_spread(offset, carried, target=target, second=second, arrive=arrive):
            arrive(offset, carried)
            slot = peer("lat", lat_count, -offset)
            for ahead in range(1, lon_count):
                spread_copy(target, slot, second, ahead, offset, lon_count).start()
            return carried

        lax.fori_loop(1, counts[axis], arrive_and_spread if kind == "spread" else arrive, 0)
    for kind, axis, source, landing, target, own, first, second in plans:

        def leave(offset, carried, plan=(source, landing, first, axis, counts[axis])):
            swap_copy(*plan, offset).wait_send()
            return carried

        lax.fori_loop(1, counts[axis], leave, 0)
        if kind == "spread":

            def finish(offset, carried, target=target, second=second):
                slot = peer("lat", lat_count, -offset)
                for ahead in range(1, lon_count):
                    copy = spread_copy(target, slot, second, ahead, offset, lon_count)
                    copy.wait_send()
                    copy.wait_recv()
                return carried

            lax.fori_loop(0, lat_count, finish, 0)


def exchange(ident, *pairs):
    counts = {"lat": lax.axis_size("lat"), "lon": lax.axis_size("lon")}
    kinds = [kind for kind, _ in pairs]
    arrays = [array for _, array in pairs]
    shapes, scratch = [], []
    for kind, array in pairs:
        shape = (counts["lon"],) + array.shape if kind == "spread" else array.shape
        shapes.append(jax.ShapeDtypeStruct(shape, array.dtype))
        axis = "lat" if kind == "spread" else kind
        scratch.append(pltpu.SemaphoreType.DMA)
        scratch.append(pltpu.SemaphoreType.DMA((2, counts[axis])))
        further = (2, counts["lon"], counts["lat"]) if kind == "spread" else (1,)
        scratch.append(pltpu.SemaphoreType.DMA(further))
    return pl.pallas_call(
        functools.partial(exchange_kernel, kinds, counts),
        out_shape=shapes,
        in_specs=[ANY] * len(arrays),
        out_specs=[ANY] * len(arrays),
        scratch_shapes=scratch,
        compiler_params=limits(collective_id=ident, has_side_effects=True),
    )(*arrays)


PAIR = 2


def spectrum_kernel(lon_count, scale_ref, table_ref, field_ref, out_ref):
    _, lat_count, depth, width = out_ref.shape
    step = pl.program_id(0)
    parts = []
    for row in range(PAIR):
        part = jnp.dot(table_ref[...], field_ref[row], preferred_element_type=jnp.float32)
        parts.append(part * scale_ref[step * PAIR + row])
    for owner in range(lon_count):
        piece = [
            part[:, owner * width : (owner + 1) * width].reshape(lat_count, depth // PAIR, width)
            for part in parts
        ]
        out_ref[owner] = jnp.concatenate(piece, axis=1).astype(jnp.bfloat16)


def partial_spectrum(field, table, scale, lat_count, lon_count):
    rows, points, channels = field.shape
    orders = table.shape[0] // lat_count
    width = channels // lon_count
    block = (lon_count, lat_count, PAIR * orders, width)
    return pl.pallas_call(
        functools.partial(spectrum_kernel, lon_count),
        grid=(rows // PAIR,),
        out_shape=jax.ShapeDtypeStruct(
            (lon_count, lat_count, rows * orders, width), jnp.bfloat16
        ),
        in_specs=[
            SMEM,
            pl.BlockSpec(table.shape, lambda i: (0, 0)),
            pl.BlockSpec((PAIR, points, channels), lambda i: (i, 0, 0)),
        ],
        out_specs=pl.BlockSpec(block, lambda i: (0, 0, i, 0)),
        compiler_params=limits(),
    )(scale, table, field)


def transform_kernel(forward, legendre_ref, scale_ref, in_ref, out_ref, in_rows, out_rows):
    orders, degrees, count_lat = legendre_ref.shape
    taken, given = (count_lat, degrees) if forward else (degrees, count_lat)
    width = in_ref.shape[1]
    in_rows[...] = in_ref[...].astype(jnp.float32)
    for order in range(orders):
        piece = [in_rows[pl.ds(2 * order + r, taken, stride=2 * orders), :] for r in range(2)]
        value = lax.dot_general(
            legendre_ref[order],
            jnp.concatenate(piece, axis=1).astype(jnp.bfloat16),
            (((1 if forward else 0,), (0,)), ((), ())),
            preferred_element_type=jnp.float32,
        )
        if not forward:
            value = value * scale_ref[...]
        for r in range(2):
            out_rows[pl.ds(2 * order + r, given, stride=2 * orders), :] = value[
                :, r * width : (r + 1) * width
            ]
    out_ref[...] = out_rows[...].astype(jnp.bfloat16)


def transform(forward, legendre, scale, rows):
    orders, degrees, count_lat = legendre.shape
    height = 2 * orders * (degrees if forward else count_lat)
    return pl.pallas_call(
        functools.partial(transform_kernel, forward),
        out_shape=jax.ShapeDtypeStruct((height, rows.shape[1]), jnp.bfloat16),
        in_specs=[VMEM] * 3,
        out_specs=VMEM,
        scratch_shapes=[
            pltpu.VMEM(rows.shape, jnp.float32),
            pltpu.VMEM((height, rows.shape[1]), jnp.float32),
        ],
        compiler_params=limits(),
    )(legendre, scale, rows)


def degree_rows(ref, lead, pair, depth):
    block = ref[lead + (slice(None), slice(pair * PAIR * depth, (pair + 1) * PAIR * depth))]
    block = block.astype(jnp.float32)
    count, _, width = block.shape
    return [
        block[:, i * depth : (i + 1) * depth].reshape(count * depth, width).astype(jnp.bfloat16)
        for i in range(PAIR)
    ]


def all_channels(ref, pair, depth):
    owners = [degree_rows(ref, (o,), pair, depth) for o in range(ref.shape[0])]
    return [jnp.concatenate([rows[i] for rows in owners], axis=1) for i in range(PAIR)]


def mix_kernel(adjoint_ref, mixing_ref, out_ref):
    degrees, width = mixing_ref.shape[:2]
    _, lat_count, height, _ = adjoint_ref.shape
    depth = height // degrees
    for pair in range(degrees // PAIR):
        values = []
        for i, full in enumerate(all_channels(adjoint_ref, pair, depth)):
            value = lax.dot_general(
                full,
                mixing_ref[pair * PAIR + i],
                (((1,), (1,)), ((), ())),
                preferred_element_type=jnp.float32,
            )
            values.append(value.reshape(lat_count, depth, width))
        out_ref[:, pair * PAIR * depth : (pair + 1) * PAIR * depth, :] = jnp.concatenate(
            values, axis=1
        ).astype(jnp.bfloat16)


def mix(adjoint, mixing):
    return pl.pallas_call(
        mix_kernel,
        out_shape=jax.ShapeDtypeStruct(adjoint.shape[1:], jnp.bfloat16),
        in_specs=[VMEM] * 2,
        out_specs=VMEM,
        compiler_params=limits(),
    )(adjoint, mixing)


def weight_kernel(adjoint_ref, coefficient_ref, out_ref):
    degrees = out_ref.shape[0]
    depth = adjoint_ref.shape[2] // degrees
    for pair in range(degrees // PAIR):
        full = all_channels(adjoint_ref, pair, depth)
        own = degree_rows(coefficient_ref, (), pair, depth)
        for i in range(PAIR):
            out_ref[pair * PAIR + i] = lax.dot_general(
                own[i], full[i], (((0,), (0,)), ((), ())), preferred_element_type=jnp.float32
            )


def weight_gradient(adjoint, coefficients, degrees):
    lon_count, _, _, width = adjoint.shape
    return pl.pallas_call(
        weight_kernel,
        out_shape=jax.ShapeDtypeStruct((degrees, width, lon_count * width), jnp.float32),
        in_specs=[VMEM] * 2,
        out_specs=VMEM,
        compiler_params=limits(),
    )(adjoint, coefficients)


def grid_kernel(table_ref, back_ref, field_ref, out_ref):
    lon_count, lat_count, height, width = back_ref.shape
    depth = height // PAIR
    back = back_ref[...].astype(jnp.float32)
    for row in range(PAIR):
        piece = [
            back[o, :, row * depth : (row + 1) * depth, :].reshape(lat_count * depth, width)
            for o in range(lon_count)
        ]
        full = jnp.concatenate(piece, axis=1).astype(jnp.bfloat16)
        value = jnp.dot(table_ref[...], full, preferred_element_type=jnp.float32)
        value = value.astype(jnp.bfloat16).astype(jnp.float32)
        out_ref[row] = (field_ref[row].astype(jnp.float32) + value).astype(jnp.bfloat16)


def grid_gradient(table, back, field):
    rows, points, channels = field.shape
    lon_count, lat_count, height, width = back.shape
    block = (PAIR, points, channels)
    return pl.pallas_call(
        grid_kernel,
        grid=(rows // PAIR,),
        out_shape=jax.ShapeDtypeStruct(field.shape, jnp.bfloat16),
        in_specs=[
            pl.BlockSpec(table.shape, lambda i: (0, 0)),
            pl.BlockSpec(
                (lon_count, lat_count, height // (rows // PAIR), width), lambda i: (0, 0, i, 0)
            ),
            pl.BlockSpec(block, lambda i: (i, 0, 0)),
        ],
        out_specs=pl.BlockSpec(block, lambda i: (i, 0, 0)),
        compiler_params=limits(),
    )(table, back, field)


def add_parts(parts):
    return jnp.sum(parts.astype(jnp.float32), axis=0).astype(jnp.bfloat16)


def local(grid_input, cotangent, mixing):
    lat_count = lax.axis_size("lat")
    lon_count = lax.axis_size("lon")
    lat_rows, lon_rows, channels = grid_input.shape
    count_lat = lat_rows * lat_count
    count_lon = lon_rows * lon_count
    per_dev = mixing.shape[0]
    order_total = per_dev * lat_count
    block_ch = channels // lon_count
    lat_pos = lax.axis_index("lat")
    lon_pos = lax.axis_index("lon")
    slot_ids = jnp.arange(order_total, dtype=jnp.int32)
    forward, backward = fourier_tables(slot_ids, lon_pos * lon_rows, lon_rows, count_lon)
    weights = quadrature(count_lat)
    own_weights = lax.dynamic_slice_in_dim(weights, lat_pos * lat_rows, lat_rows)
    own_orders = lat_pos * per_dev + jnp.arange(per_dev, dtype=jnp.int32)
    legendre = legendre_table(own_orders, count_lat, order_total, order_total)
    scale = weights[:, None]
    by_lat = (lat_count, -1, block_ch)
    flat = (-1, block_ch)

    part_g = partial_spectrum(
        cotangent, backward.T, jnp.ones_like(own_weights), lat_count, lon_count
    )
    (part_g,) = exchange(0, ("lon", part_g))
    part_x = partial_spectrum(grid_input, forward.T, own_weights, lat_count, lon_count)
    part_x, rows_g = exchange(1, ("lon", part_x), ("lat", add_parts(part_g)))
    adjoint = transform(True, legendre, scale, rows_g.reshape(flat))
    (adjoint,) = exchange(2, ("spread", adjoint.reshape(by_lat)))
    mixed = mix(adjoint, mixing)
    mixed, rows_x = exchange(3, ("lat", mixed), ("lat", add_parts(part_x)))
    back = transform(False, legendre, scale, mixed.reshape(flat))
    coefficients = transform(True, legendre, scale, rows_x.reshape(flat))
    back, coefficients = exchange(
        4, ("spread", back.reshape(by_lat)), ("lat", coefficients.reshape(by_lat))
    )
    input_grad = grid_gradient(forward, back, cotangent)
    weight_grad = weight_gradient(adjoint, coefficients, per_dev)
    return (input_grad, weight_grad)


def solution(mesh):
    in_specs = (P("lat", "lon", None), P("lat", "lon", None), P("lat", "lon", None))
    out_specs = (P("lat", "lon", None), P("lat", "lon", None))
    return jax.shard_map(local, mesh=mesh, in_specs=in_specs, out_specs=out_specs, check_vma=False)
```

```python
import functools
import math

import jax
import jax.numpy as jnp
from jax import lax
from jax.experimental import pallas as pl
from jax.experimental.pallas import tpu as pltpu
from jax.sharding import PartitionSpec as P


def quadrature(count_lat):
    colatitude = (jnp.arange(count_lat, dtype=jnp.float32) + 0.5) * (math.pi / count_lat)
    return math.pi / count_lat * jnp.sin(colatitude)


BLOCK = 16


def legendre_kernel(order_ref, cosine_ref, start_ref, out_ref, rows_ref):
    order = order_ref[...]
    cosine = cosine_ref[...]
    first_scale = jnp.sqrt(2.0 * order + 3.0)

    def advance(degree, carried):
        previous, earlier, scale_log = carried
        growth = jnp.sqrt(
            (4.0 * degree * degree - 1.0) / jnp.maximum(degree * degree - order * order, 1.0)
        )
        below = (degree - 1.0) * (degree - 1.0)
        shrink = jnp.sqrt(
            jnp.maximum(below - order * order, 0.0) / jnp.maximum(4.0 * below - 1.0, 1.0)
        )
        growth = jnp.where(degree == order + 1.0, first_scale, growth)
        growth = jnp.where(degree > order, growth, 0.0)
        current = growth * (cosine * previous - shrink * earlier)
        current = jnp.where(degree == order, 1.0, current)
        oversized = jnp.abs(current) > 10000000000.0
        factor = jnp.where(oversized, 1e-10, 1.0)
        scale_log = scale_log + jnp.where(oversized, math.log(10000000000.0), 0.0)
        current = current * factor
        return (current, previous * factor, scale_log), current * jnp.exp(scale_log)

    def block(index, carried):
        base = index * BLOCK
        for step in range(BLOCK):
            degree = (base + step).astype(jnp.float32)
            carried, value = advance(degree, carried)
            rows_ref[:, step, :] = value
        out_ref[:, pl.ds(pl.multiple_of(base, BLOCK), BLOCK), :] = rows_ref[...].astype(
            jnp.bfloat16
        )
        return carried

    zero = jnp.zeros(start_ref.shape, jnp.float32)
    lax.fori_loop(0, out_ref.shape[1] // BLOCK, block, (zero, zero, start_ref[...]))


def legendre_table(order_ids, count_lat, degrees, order_cap):
    colatitude = (jnp.arange(count_lat, dtype=jnp.float32) + 0.5) * (math.pi / count_lat)
    cosine = jnp.cos(colatitude)[None, :]
    sine_row = jnp.sin(colatitude)[None, :]
    order_value = order_ids.astype(jnp.float32)[:, None]
    counter = jnp.arange(1, order_cap + 1, dtype=jnp.float32)[None, :]
    log_terms = jnp.where(counter <= order_value, jnp.log1p(0.5 / counter), 0.0)
    log_start = (
        0.5 * math.log(0.5)
        + 0.5 * jnp.sum(log_terms, axis=1, keepdims=True)
        + order_value * jnp.log(sine_row)
    )
    orders = order_ids.shape[0]
    return pl.pallas_call(
        legendre_kernel,
        out_shape=jax.ShapeDtypeStruct((orders, degrees, count_lat), jnp.bfloat16),
        in_specs=[pl.BlockSpec(memory_space=pltpu.VMEM)] * 3,
        out_specs=pl.BlockSpec(memory_space=pltpu.VMEM),
        scratch_shapes=[pltpu.VMEM((orders, BLOCK, count_lat), jnp.float32)],
        compiler_params=pltpu.CompilerParams(vmem_limit_bytes=48 * 1024 * 1024),
    )(order_value, cosine, log_start)


def fourier_tables(order_ids, first, points_held, count_lon):
    points = first + jnp.arange(points_held, dtype=jnp.int32)
    phase_index = points[:, None] * order_ids[None, :] % count_lon
    angles = phase_index.astype(jnp.float32) * (2.0 * math.pi / count_lon)
    forward = jnp.stack([jnp.cos(angles), -jnp.sin(angles)], axis=2).reshape(
        points_held, 2 * order_ids.shape[0]
    )
    factor = jnp.where(order_ids == 0, 1.0, 2.0).astype(jnp.float32) / count_lon
    backward = forward * jnp.repeat(factor, 2)[None, :]
    return (forward.astype(jnp.bfloat16), backward.astype(jnp.bfloat16))


MESH = pl.DeviceIdType.MESH
VMEM = pl.BlockSpec(memory_space=pltpu.VMEM)
SMEM = pl.BlockSpec(memory_space=pltpu.SMEM)
ANY = pl.BlockSpec(memory_space=pl.ANY)


def limits(**more):
    return pltpu.CompilerParams(vmem_limit_bytes=48 * 1024 * 1024, **more)


def peer(axis, count, offset):
    return lax.rem(lax.axis_index(axis) + offset + count, count)


class Swap:
    def __init__(self, counts, source, target, landing, own_sem, sems):
        self.counts, self.source, self.target = counts, source, target
        self.landing, self.sems = landing, sems
        self.here = lax.axis_index("lat")
        self.own = pltpu.make_async_copy(
            source.at[self.here], landing.at[self.here], own_sem
        )

    def copy(self, offset):
        there = peer("lat", self.counts["lat"], offset)
        return pltpu.make_async_remote_copy(
            src_ref=self.source.at[there],
            dst_ref=self.landing.at[self.here],
            send_sem=self.sems.at[0, offset],
            recv_sem=self.sems.at[1, offset],
            device_id={"lat": there},
            device_id_type=MESH,
        )

    def each(self, act):
        def body(offset, carried):
            act(self.copy(offset))
            return carried

        lax.fori_loop(1, self.counts["lat"], body, 0)

    def start(self):
        self.each(lambda copy: copy.start())
        self.own.start()

    def first(self):
        pass

    def step(self, offset):
        pass

    def finish(self):
        self.own.wait()
        self.each(lambda copy: copy.wait())


class Spread(Swap):
    def __init__(self, counts, source, target, own_sem, sems, further):
        super().__init__(
            counts, source, target, target.at[lax.axis_index("lon")], own_sem, sems
        )
        self.further = further

    def onward(self, offset, ahead):
        slot = peer("lat", self.counts["lat"], -offset)
        return pltpu.make_async_remote_copy(
            src_ref=self.landing.at[slot],
            dst_ref=self.landing.at[slot],
            send_sem=self.further.at[0, ahead, offset],
            recv_sem=self.further.at[1, ahead, offset],
            device_id={"lon": peer("lon", self.counts["lon"], ahead)},
            device_id_type=MESH,
        )

    def first(self):
        self.own.wait()
        for ahead in range(1, self.counts["lon"]):
            self.onward(0, ahead).start()

    def step(self, offset):
        self.copy(offset).wait_recv()
        for ahead in range(1, self.counts["lon"]):
            self.onward(offset, ahead).start()

    def finish(self):
        self.each(lambda copy: copy.wait_send())

        def body(offset, carried):
            for ahead in range(1, self.counts["lon"]):
                self.onward(offset, ahead).wait()
            return carried

        lax.fori_loop(0, self.counts["lat"], body, 0)


class Reduce(Swap):
    def __init__(self, counts, source, target, own_sem, sems, further, sums, arrived, load_sem):
        super().__init__(counts, sums, target, target, own_sem, sems)
        self.parts, self.further, self.sums, self.arrived = source, further, sums, arrived
        self.load = pltpu.make_async_copy(source.at[lax.axis_index("lon")], sums, load_sem)

    def across(self, offset, ahead):
        slot = peer("lat", self.counts["lat"], offset)
        there = peer("lon", self.counts["lon"], ahead)
        return pltpu.make_async_remote_copy(
            src_ref=self.parts.at[there, slot],
            dst_ref=self.arrived.at[ahead - 1, slot],
            send_sem=self.further.at[0, ahead, offset],
            recv_sem=self.further.at[1, ahead, offset],
            device_id={"lon": there},
            device_id_type=MESH,
        )

    def every(self, begin, act):
        def body(offset, carried):
            for ahead in range(1, self.counts["lon"]):
                act(self.across(offset, ahead))
            return carried

        lax.fori_loop(begin, self.counts["lat"], body, 0)

    def start(self):
        self.load.start()
        self.every(1, lambda copy: copy.start())
        for ahead in range(1, self.counts["lon"]):
            self.across(0, ahead).start()

    def first(self):
        self.load.wait()

    def add(self, offset):
        slot = peer("lat", self.counts["lat"], offset)
        total = self.sums[slot].astype(jnp.float32)
        for ahead in range(1, self.counts["lon"]):
            self.across(offset, ahead).wait_recv()
            total = total + self.arrived[ahead - 1, slot].astype(jnp.float32)
        self.sums[slot] = total.astype(jnp.bfloat16)

    def step(self, offset):
        self.add(offset)
        self.copy(offset).start()

    def finish(self):
        self.add(0)
        self.own.start()
        self.own.wait()
        self.each(lambda copy: copy.wait())
        self.every(0, lambda copy: copy.wait_send())


def exchange_kernel(kinds, counts, lengths, *refs):
    total = len(kinds)
    sources, targets, scratch = refs[:total], refs[total : 2 * total], refs[2 * total :]

    barrier = pltpu.get_barrier_semaphore()
    expected = 0
    for axis in ("lon", "lat") if set(kinds) != {Swap} else ("lat",):

        def greet(offset, carried, axis=axis):
            there = peer(axis, counts[axis], offset)
            pl.semaphore_signal(barrier, inc=1, device_id={axis: there}, device_id_type=MESH)
            return carried

        lax.fori_loop(1, counts[axis], greet, 0)
        expected += counts[axis] - 1
    pl.semaphore_wait(barrier, expected)

    jobs, place = [], 0
    for kind, length, source, target in zip(kinds, lengths, sources, targets):
        held = scratch[place : place + length]
        landing = (target,) if kind is Swap else ()
        jobs.append(kind(counts, source, target, *landing, *held))
        place += length
    for job in jobs:
        job.start()
    for job in jobs:
        job.first()

    if set(kinds) != {Swap}:

        def body(offset, carried):
            for job in jobs:
                job.step(offset)
            return carried

        lax.fori_loop(1, counts["lat"], body, 0)
    for job in jobs:
        job.finish()


def exchange(ident, *pairs):
    counts = {"lat": lax.axis_size("lat"), "lon": lax.axis_size("lon")}
    kinds = [kind for kind, _ in pairs]
    arrays = [array for _, array in pairs]
    dma = pltpu.SemaphoreType.DMA
    shapes, scratch, lengths = [], [], []
    for kind, array in pairs:
        shape = array.shape
        held = [dma, dma((2, counts["lat"]))]
        if kind is not Swap:
            held.append(dma((2, counts["lon"], counts["lat"])))
        if kind is Spread:
            shape = (counts["lon"],) + shape
        if kind is Reduce:
            shape = shape[1:]
            held.append(pltpu.VMEM(shape, array.dtype))
            held.append(pltpu.VMEM((counts["lon"] - 1,) + shape, array.dtype))
            held.append(dma)
        shapes.append(jax.ShapeDtypeStruct(shape, array.dtype))
        scratch += held
        lengths.append(len(held))
    return pl.pallas_call(
        functools.partial(exchange_kernel, kinds, counts, lengths),
        out_shape=shapes,
        in_specs=[ANY] * len(arrays),
        out_specs=[ANY] * len(arrays),
        scratch_shapes=scratch,
        compiler_params=limits(collective_id=ident, has_side_effects=True),
    )(*arrays)


PAIR = 2


def spectrum_kernel(lon_count, scale_ref, table_ref, field_ref, out_ref):
    _, lat_count, depth, width = out_ref.shape
    step = pl.program_id(0)
    parts = []
    for row in range(PAIR):
        part = jnp.dot(table_ref[...], field_ref[row], preferred_element_type=jnp.float32)
        parts.append(part * scale_ref[step * PAIR + row])
    for owner in range(lon_count):
        piece = [
            part[:, owner * width : (owner + 1) * width].reshape(lat_count, depth // PAIR, width)
            for part in parts
        ]
        out_ref[owner] = jnp.concatenate(piece, axis=1).astype(jnp.bfloat16)


def partial_spectrum(field, table, scale, lat_count, lon_count):
    rows, points, channels = field.shape
    orders = table.shape[0] // lat_count
    width = channels // lon_count
    block = (lon_count, lat_count, PAIR * orders, width)
    return pl.pallas_call(
        functools.partial(spectrum_kernel, lon_count),
        grid=(rows // PAIR,),
        out_shape=jax.ShapeDtypeStruct(
            (lon_count, lat_count, rows * orders, width), jnp.bfloat16
        ),
        in_specs=[
            SMEM,
            pl.BlockSpec(table.shape, lambda i: (0, 0)),
            pl.BlockSpec((PAIR, points, channels), lambda i: (i, 0, 0)),
        ],
        out_specs=pl.BlockSpec(block, lambda i: (0, 0, i, 0)),
        compiler_params=limits(),
    )(scale, table, field)


def transform_kernel(forward, legendre_ref, scale_ref, in_ref, out_ref, in_rows, out_rows):
    orders, degrees, count_lat = legendre_ref.shape
    taken, given = (count_lat, degrees) if forward else (degrees, count_lat)
    width = in_ref.shape[1]
    in_rows[...] = in_ref[...].astype(jnp.float32)
    for order in range(orders):
        piece = [in_rows[pl.ds(2 * order + r, taken, stride=2 * orders), :] for r in range(2)]
        value = lax.dot_general(
            legendre_ref[order],
            jnp.concatenate(piece, axis=1).astype(jnp.bfloat16),
            (((1 if forward else 0,), (0,)), ((), ())),
            preferred_element_type=jnp.float32,
        )
        if not forward:
            value = value * scale_ref[...]
        for r in range(2):
            out_rows[pl.ds(2 * order + r, given, stride=2 * orders), :] = value[
                :, r * width : (r + 1) * width
            ]
    out_ref[...] = out_rows[...].astype(jnp.bfloat16)


def transform(forward, legendre, scale, rows):
    orders, degrees, count_lat = legendre.shape
    height = 2 * orders * (degrees if forward else count_lat)
    return pl.pallas_call(
        functools.partial(transform_kernel, forward),
        out_shape=jax.ShapeDtypeStruct((height, rows.shape[1]), jnp.bfloat16),
        in_specs=[VMEM] * 3,
        out_specs=VMEM,
        scratch_shapes=[
            pltpu.VMEM(rows.shape, jnp.float32),
            pltpu.VMEM((height, rows.shape[1]), jnp.float32),
        ],
        compiler_params=limits(),
    )(legendre, scale, rows)


def degree_rows(ref, lead, pair, depth):
    block = ref[lead + (slice(None), slice(pair * PAIR * depth, (pair + 1) * PAIR * depth))]
    block = block.astype(jnp.float32)
    count, _, width = block.shape
    return [
        block[:, i * depth : (i + 1) * depth].reshape(count * depth, width).astype(jnp.bfloat16)
        for i in range(PAIR)
    ]


def all_channels(ref, pair, depth):
    owners = [degree_rows(ref, (o,), pair, depth) for o in range(ref.shape[0])]
    return [jnp.concatenate([rows[i] for rows in owners], axis=1) for i in range(PAIR)]


def mix_kernel(adjoint_ref, mixing_ref, out_ref):
    degrees, width = mixing_ref.shape[:2]
    _, lat_count, height, _ = adjoint_ref.shape
    depth = height // degrees
    for pair in range(degrees // PAIR):
        values = []
        for i, full in enumerate(all_channels(adjoint_ref, pair, depth)):
            value = lax.dot_general(
                full,
                mixing_ref[pair * PAIR + i],
                (((1,), (1,)), ((), ())),
                preferred_element_type=jnp.float32,
            )
            values.append(value.reshape(lat_count, depth, width))
        out_ref[:, pair * PAIR * depth : (pair + 1) * PAIR * depth, :] = jnp.concatenate(
            values, axis=1
        ).astype(jnp.bfloat16)


def mix(adjoint, mixing):
    return pl.pallas_call(
        mix_kernel,
        out_shape=jax.ShapeDtypeStruct(adjoint.shape[1:], jnp.bfloat16),
        in_specs=[VMEM] * 2,
        out_specs=VMEM,
        compiler_params=limits(),
    )(adjoint, mixing)


def weight_kernel(adjoint_ref, coefficient_ref, out_ref):
    degrees = out_ref.shape[0]
    depth = adjoint_ref.shape[2] // degrees
    for pair in range(degrees // PAIR):
        full = all_channels(adjoint_ref, pair, depth)
        own = degree_rows(coefficient_ref, (), pair, depth)
        for i in range(PAIR):
            out_ref[pair * PAIR + i] = lax.dot_general(
                own[i], full[i], (((0,), (0,)), ((), ())), preferred_element_type=jnp.float32
            )


def weight_gradient(adjoint, coefficients, degrees):
    lon_count, _, _, width = adjoint.shape
    return pl.pallas_call(
        weight_kernel,
        out_shape=jax.ShapeDtypeStruct((degrees, width, lon_count * width), jnp.float32),
        in_specs=[VMEM] * 2,
        out_specs=VMEM,
        compiler_params=limits(),
    )(adjoint, coefficients)


def grid_kernel(table_ref, back_ref, field_ref, out_ref):
    lon_count, lat_count, height, width = back_ref.shape
    depth = height // PAIR
    back = back_ref[...].astype(jnp.float32)
    for row in range(PAIR):
        piece = [
            back[o, :, row * depth : (row + 1) * depth, :].reshape(lat_count * depth, width)
            for o in range(lon_count)
        ]
        full = jnp.concatenate(piece, axis=1).astype(jnp.bfloat16)
        value = jnp.dot(table_ref[...], full, preferred_element_type=jnp.float32)
        value = value.astype(jnp.bfloat16).astype(jnp.float32)
        out_ref[row] = (field_ref[row].astype(jnp.float32) + value).astype(jnp.bfloat16)


def grid_gradient(table, back, field):
    rows, points, channels = field.shape
    lon_count, lat_count, height, width = back.shape
    block = (PAIR, points, channels)
    return pl.pallas_call(
        grid_kernel,
        grid=(rows // PAIR,),
        out_shape=jax.ShapeDtypeStruct(field.shape, jnp.bfloat16),
        in_specs=[
            pl.BlockSpec(table.shape, lambda i: (0, 0)),
            pl.BlockSpec(
                (lon_count, lat_count, height // (rows // PAIR), width), lambda i: (0, 0, i, 0)
            ),
            pl.BlockSpec(block, lambda i: (i, 0, 0)),
        ],
        out_specs=pl.BlockSpec(block, lambda i: (i, 0, 0)),
        compiler_params=limits(),
    )(table, back, field)


def local(grid_input, cotangent, mixing):
    lat_count = lax.axis_size("lat")
    lon_count = lax.axis_size("lon")
    lat_rows, lon_rows, channels = grid_input.shape
    count_lat = lat_rows * lat_count
    count_lon = lon_rows * lon_count
    per_dev = mixing.shape[0]
    order_total = per_dev * lat_count
    block_ch = channels // lon_count
    lat_pos = lax.axis_index("lat")
    lon_pos = lax.axis_index("lon")
    slot_ids = jnp.arange(order_total, dtype=jnp.int32)
    forward, backward = fourier_tables(slot_ids, lon_pos * lon_rows, lon_rows, count_lon)
    weights = quadrature(count_lat)
    own_weights = lax.dynamic_slice_in_dim(weights, lat_pos * lat_rows, lat_rows)
    own_orders = lat_pos * per_dev + jnp.arange(per_dev, dtype=jnp.int32)
    legendre = legendre_table(own_orders, count_lat, order_total, order_total)
    scale = weights[:, None]
    by_lat = (lat_count, -1, block_ch)
    flat = (-1, block_ch)

    part_g = partial_spectrum(
        cotangent, backward.T, jnp.ones_like(own_weights), lat_count, lon_count
    )
    (rows_g,) = exchange(0, (Reduce, part_g))
    part_x = partial_spectrum(grid_input, forward.T, own_weights, lat_count, lon_count)
    adjoint = transform(True, legendre, scale, rows_g.reshape(flat))
    adjoint, rows_x = exchange(1, (Spread, adjoint.reshape(by_lat)), (Reduce, part_x))
    (mixed,) = exchange(2, (Swap, mix(adjoint, mixing)))
    back = transform(False, legendre, scale, mixed.reshape(flat))
    coefficients = transform(True, legendre, scale, rows_x.reshape(flat))
    back, coefficients = exchange(
        3, (Spread, back.reshape(by_lat)), (Swap, coefficients.reshape(by_lat))
    )
    input_grad = grid_gradient(forward, back, cotangent)
    weight_grad = weight_gradient(adjoint, coefficients, per_dev)
    return (input_grad, weight_grad)


def solution(mesh):
    in_specs = (P("lat", "lon", None), P("lat", "lon", None), P("lat", "lon", None))
    out_specs = (P("lat", "lon", None), P("lat", "lon", None))
    return jax.shard_map(local, mesh=mesh, in_specs=in_specs, out_specs=out_specs, check_vma=False)
```

```python
import functools
import math

import jax
import jax.numpy as jnp
from jax import lax
from jax.experimental import pallas as pl
from jax.experimental.pallas import tpu as pltpu
from jax.sharding import PartitionSpec as P


def quadrature(count_lat):
    colatitude = (jnp.arange(count_lat, dtype=jnp.float32) + 0.5) * (math.pi / count_lat)
    return math.pi / count_lat * jnp.sin(colatitude)


BLOCK = 16


def legendre_kernel(order_ref, cosine_ref, start_ref, out_ref, rows_ref):
    order = order_ref[...]
    cosine = cosine_ref[...]
    first_scale = jnp.sqrt(2.0 * order + 3.0)

    def advance(degree, carried):
        previous, earlier, scale_log = carried
        growth = jnp.sqrt(
            (4.0 * degree * degree - 1.0) / jnp.maximum(degree * degree - order * order, 1.0)
        )
        below = (degree - 1.0) * (degree - 1.0)
        shrink = jnp.sqrt(
            jnp.maximum(below - order * order, 0.0) / jnp.maximum(4.0 * below - 1.0, 1.0)
        )
        growth = jnp.where(degree == order + 1.0, first_scale, growth)
        growth = jnp.where(degree > order, growth, 0.0)
        current = growth * (cosine * previous - shrink * earlier)
        current = jnp.where(degree == order, 1.0, current)
        oversized = jnp.abs(current) > 10000000000.0
        factor = jnp.where(oversized, 1e-10, 1.0)
        scale_log = scale_log + jnp.where(oversized, math.log(10000000000.0), 0.0)
        current = current * factor
        return (current, previous * factor, scale_log), current * jnp.exp(scale_log)

    def block(index, carried):
        base = index * BLOCK
        for step in range(BLOCK):
            degree = (base + step).astype(jnp.float32)
            carried, value = advance(degree, carried)
            rows_ref[:, step, :] = value
        out_ref[:, pl.ds(pl.multiple_of(base, BLOCK), BLOCK), :] = rows_ref[...].astype(
            jnp.bfloat16
        )
        return carried

    zero = jnp.zeros(start_ref.shape, jnp.float32)
    lax.fori_loop(0, out_ref.shape[1] // BLOCK, block, (zero, zero, start_ref[...]))


def legendre_table(order_ids, count_lat, degrees, order_cap):
    colatitude = (jnp.arange(count_lat, dtype=jnp.float32) + 0.5) * (math.pi / count_lat)
    cosine = jnp.cos(colatitude)[None, :]
    sine_row = jnp.sin(colatitude)[None, :]
    order_value = order_ids.astype(jnp.float32)[:, None]
    counter = jnp.arange(1, order_cap + 1, dtype=jnp.float32)[None, :]
    log_terms = jnp.where(counter <= order_value, jnp.log1p(0.5 / counter), 0.0)
    log_start = (
        0.5 * math.log(0.5)
        + 0.5 * jnp.sum(log_terms, axis=1, keepdims=True)
        + order_value * jnp.log(sine_row)
    )
    orders = order_ids.shape[0]
    return pl.pallas_call(
        legendre_kernel,
        out_shape=jax.ShapeDtypeStruct((orders, degrees, count_lat), jnp.bfloat16),
        in_specs=[pl.BlockSpec(memory_space=pltpu.VMEM)] * 3,
        out_specs=pl.BlockSpec(memory_space=pltpu.VMEM),
        scratch_shapes=[pltpu.VMEM((orders, BLOCK, count_lat), jnp.float32)],
        compiler_params=pltpu.CompilerParams(vmem_limit_bytes=48 * 1024 * 1024),
    )(order_value, cosine, log_start)


def fourier_tables(order_ids, first, points_held, count_lon):
    def angles(order, part, point):
        index = 4 * (point * order) + part * count_lon
        return (index % (4 * count_lon)).astype(jnp.float32) * (0.5 * math.pi / count_lon)

    points = first + jnp.arange(points_held, dtype=jnp.int32)
    slots = jnp.repeat(order_ids, 2)
    parts = jnp.arange(slots.shape[0], dtype=jnp.int32) % 2
    forward = jnp.cos(angles(slots[None, :], parts[None, :], points[:, None]))
    forward_rows = jnp.cos(angles(slots[:, None], parts[:, None], points[None, :]))
    factor = jnp.where(slots == 0, 1.0, 2.0).astype(jnp.float32) / count_lon
    tables = (forward, forward_rows, forward_rows * factor[:, None])
    return tuple(table.astype(jnp.bfloat16) for table in tables)


MESH = pl.DeviceIdType.MESH
VMEM = pl.BlockSpec(memory_space=pltpu.VMEM)
SMEM = pl.BlockSpec(memory_space=pltpu.SMEM)
ANY = pl.BlockSpec(memory_space=pl.ANY)


def limits(**more):
    return pltpu.CompilerParams(vmem_limit_bytes=48 * 1024 * 1024, **more)


def peer(axis, count, offset):
    return lax.rem(lax.axis_index(axis) + offset + count, count)


class Swap:
    def __init__(self, counts, reach, source, target, landing, own_sem, sems):
        self.counts, self.reach, self.source, self.target = counts, reach, source, target
        self.landing, self.sems = landing, sems
        self.here = lax.axis_index("lat")
        self.chunks = sems.shape[2]
        self.own = pltpu.make_async_copy(
            source.at[self.here], landing.at[self.here], own_sem
        )

    def rows(self, chunk):
        height = self.landing.shape[1] // self.chunks
        return pl.ds(chunk * height, height)

    def copy(self, offset, chunk):
        there = peer("lat", self.counts["lat"], offset)
        return pltpu.make_async_remote_copy(
            src_ref=self.source.at[there, self.rows(chunk)],
            dst_ref=self.landing.at[self.here, self.rows(chunk)],
            send_sem=self.sems.at[0, offset, chunk],
            recv_sem=self.sems.at[1, offset, chunk],
            device_id={"lat": there},
            device_id_type=MESH,
        )

    def each_chunk(self, sender, receiver, act):
        if self.reach is None:
            act(0)
            return
        orders, degrees = (sender, receiver) if self.reach == "out" else (receiver, sender)
        per_dev = self.counts["orders"]
        for chunk in range(self.chunks):
            least = orders + self.counts["lat"] * (per_dev // self.chunks) * chunk
            pl.when(least < (degrees + 1) * per_dev)(functools.partial(act, chunk))

    def send(self, offset):
        there = peer("lat", self.counts["lat"], offset)
        self.each_chunk(self.here, there, lambda chunk: self.copy(offset, chunk).start())

    def sent(self, offset):
        there = peer("lat", self.counts["lat"], offset)
        self.each_chunk(self.here, there, lambda chunk: self.copy(offset, chunk).wait_send())

    def receive(self, offset, then=None):
        origin = peer("lat", self.counts["lat"], -offset)

        def act(chunk):
            self.copy(offset, chunk).wait_recv()
            if then is not None:
                then(chunk)

        self.each_chunk(origin, self.here, act)

    def each(self, act):
        def body(offset, carried):
            act(offset)
            return carried

        lax.fori_loop(1, self.counts["lat"], body, 0)

    def start(self, alone):
        self.own.start()
        if alone:
            self.each(self.send)

    def first(self):
        pass

    def step(self, offset):
        self.send(offset)

    def finish(self):
        self.own.wait()
        self.each(self.receive)
        self.each(self.sent)


class Spread(Swap):
    def __init__(self, counts, reach, source, target, own_sem, sems, further):
        super().__init__(
            counts, reach, source, target, target.at[lax.axis_index("lon")], own_sem, sems
        )
        self.further = further

    def onward(self, offset, chunk, ahead):
        slot = peer("lat", self.counts["lat"], -offset)
        return pltpu.make_async_remote_copy(
            src_ref=self.landing.at[slot, self.rows(chunk)],
            dst_ref=self.landing.at[slot, self.rows(chunk)],
            send_sem=self.further.at[0, ahead, offset, chunk],
            recv_sem=self.further.at[1, ahead, offset, chunk],
            device_id={"lon": peer("lon", self.counts["lon"], ahead)},
            device_id_type=MESH,
        )

    def pass_on(self, offset, chunk):
        for ahead in range(1, self.counts["lon"]):
            self.onward(offset, chunk, ahead).start()

    def start(self, alone):
        self.own.start()
        self.each(self.send)

    def first(self):
        self.own.wait()
        self.each_chunk(self.here, self.here, lambda chunk: self.pass_on(0, chunk))

    def step(self, offset):
        self.receive(offset, lambda chunk: self.pass_on(offset, chunk))

    def finish(self):
        self.each(self.sent)

        def body(offset, carried):
            def act(chunk):
                for ahead in range(1, self.counts["lon"]):
                    self.onward(offset, chunk, ahead).wait()

            self.each_chunk(peer("lat", self.counts["lat"], -offset), self.here, act)
            return carried

        lax.fori_loop(0, self.counts["lat"], body, 0)


class Reduce(Swap):
    def __init__(
        self, counts, reach, source, target, own_sem, sems, further, sums, arrived, load_sem
    ):
        super().__init__(counts, None, sums, target, target, own_sem, sems)
        self.parts, self.further, self.sums, self.arrived = source, further, sums, arrived
        self.load = pltpu.make_async_copy(source.at[lax.axis_index("lon")], sums, load_sem)

    def across(self, offset, ahead):
        slot = peer("lat", self.counts["lat"], offset)
        there = peer("lon", self.counts["lon"], ahead)
        return pltpu.make_async_remote_copy(
            src_ref=self.parts.at[there, slot],
            dst_ref=self.arrived.at[ahead - 1, slot],
            send_sem=self.further.at[0, ahead, offset],
            recv_sem=self.further.at[1, ahead, offset],
            device_id={"lon": there},
            device_id_type=MESH,
        )

    def every(self, begin, act):
        def body(offset, carried):
            for ahead in range(1, self.counts["lon"]):
                act(self.across(offset, ahead))
            return carried

        lax.fori_loop(begin, self.counts["lat"], body, 0)

    def start(self, alone):
        self.load.start()
        self.every(1, lambda copy: copy.start())
        for ahead in range(1, self.counts["lon"]):
            self.across(0, ahead).start()

    def first(self):
        self.load.wait()

    def add(self, offset):
        slot = peer("lat", self.counts["lat"], offset)
        total = self.sums[slot].astype(jnp.float32)
        for ahead in range(1, self.counts["lon"]):
            self.across(offset, ahead).wait_recv()
            total = total + self.arrived[ahead - 1, slot].astype(jnp.float32)
        self.sums[slot] = total.astype(jnp.bfloat16)

    def step(self, offset):
        self.add(offset)
        self.send(offset)

    def finish(self):
        self.add(0)
        self.own.start()
        self.own.wait()
        self.each(self.receive)
        self.each(self.sent)
        self.every(0, lambda copy: copy.wait_send())


def exchange_kernel(kinds, reaches, counts, lengths, *refs):
    total = len(kinds)
    sources, targets, scratch = refs[:total], refs[total : 2 * total], refs[2 * total :]

    barrier = pltpu.get_barrier_semaphore()
    expected = 0
    for axis in ("lon", "lat") if set(kinds) != {Swap} else ("lat",):

        def greet(offset, carried, axis=axis):
            there = peer(axis, counts[axis], offset)
            pl.semaphore_signal(barrier, inc=1, device_id={axis: there}, device_id_type=MESH)
            return carried

        lax.fori_loop(1, counts[axis], greet, 0)
        expected += counts[axis] - 1
    pl.semaphore_wait(barrier, expected)

    jobs, place = [], 0
    for kind, reach, length, source, target in zip(kinds, reaches, lengths, sources, targets):
        held = scratch[place : place + length]
        landing = (target,) if kind is Swap else ()
        jobs.append(kind(counts, reach, source, target, *landing, *held))
        place += length
    for job in jobs:
        job.start(len(jobs) == 1)
    for job in jobs:
        job.first()

    if set(kinds) != {Swap}:

        def body(offset, carried):
            for job in jobs:
                job.step(offset)
            return carried

        lax.fori_loop(1, counts["lat"], body, 0)
    for job in jobs:
        job.finish()


def exchange(ident, per_dev, *jobs):
    counts = {"lat": lax.axis_size("lat"), "lon": lax.axis_size("lon"), "orders": per_dev}
    kinds = [kind for kind, _, _ in jobs]
    reaches = [reach for _, reach, _ in jobs]
    arrays = [array for _, _, array in jobs]
    dma = pltpu.SemaphoreType.DMA
    shapes, scratch, lengths = [], [], []
    for kind, reach, array in jobs:
        shape = array.shape
        chunks = 1 if reach is None else per_dev // PAIR
        while chunks % 2 == 0 and counts["lon"] * counts["lat"] * chunks > 1024:
            chunks //= 2
        held = [dma, dma((2, counts["lat"], chunks))]
        if kind is Spread:
            held.append(dma((2, counts["lon"], counts["lat"], chunks)))
        if kind is Reduce:
            held.append(dma((2, counts["lon"], counts["lat"])))
        if kind is Spread:
            shape = (counts["lon"],) + shape
        if kind is Reduce:
            shape = shape[1:]
            held.append(pltpu.VMEM(shape, array.dtype))
            held.append(pltpu.VMEM((counts["lon"] - 1,) + shape, array.dtype))
            held.append(dma)
        shapes.append(jax.ShapeDtypeStruct(shape, array.dtype))
        scratch += held
        lengths.append(len(held))
    return pl.pallas_call(
        functools.partial(exchange_kernel, kinds, reaches, counts, lengths),
        out_shape=shapes,
        in_specs=[ANY] * len(arrays),
        out_specs=[ANY] * len(arrays),
        scratch_shapes=scratch,
        compiler_params=limits(collective_id=ident, has_side_effects=True),
    )(*arrays)


PAIR = 2


def spectrum_kernel(lon_count, scale_ref, table_ref, field_ref, out_ref):
    _, lat_count, depth, width = out_ref.shape
    step = pl.program_id(0)
    parts = []
    for row in range(PAIR):
        part = jnp.dot(table_ref[...], field_ref[row], preferred_element_type=jnp.float32)
        parts.append(part * scale_ref[step * PAIR + row])
    for owner in range(lon_count):
        piece = [
            part[:, owner * width : (owner + 1) * width].reshape(lat_count, depth // PAIR, width)
            for part in parts
        ]
        out_ref[owner] = jnp.concatenate(piece, axis=1).astype(jnp.bfloat16)


def partial_spectrum(field, table, scale, lat_count, lon_count):
    rows, points, channels = field.shape
    orders = table.shape[0] // lat_count
    width = channels // lon_count
    block = (lon_count, lat_count, PAIR * orders, width)
    return pl.pallas_call(
        functools.partial(spectrum_kernel, lon_count),
        grid=(rows // PAIR,),
        out_shape=jax.ShapeDtypeStruct(
            (lon_count, lat_count, rows * orders, width), jnp.bfloat16
        ),
        in_specs=[
            SMEM,
            pl.BlockSpec(table.shape, lambda i: (0, 0)),
            pl.BlockSpec((PAIR, points, channels), lambda i: (i, 0, 0)),
        ],
        out_specs=pl.BlockSpec(block, lambda i: (0, 0, i, 0)),
        compiler_params=limits(),
    )(scale, table, field)


def analyse_kernel(legendre_ref, in_ref, out_ref, in_rows, out_rows):
    orders, degrees, count_lat = legendre_ref.shape
    width = in_ref.shape[1]
    in_rows[...] = in_ref[...].astype(jnp.float32)
    for order in range(orders):
        piece = [in_rows[pl.ds(2 * order + r, count_lat, stride=2 * orders), :] for r in range(2)]
        value = jnp.dot(
            legendre_ref[order],
            jnp.concatenate(piece, axis=1).astype(jnp.bfloat16),
            preferred_element_type=jnp.float32,
        )
        for owner in range(degrees // orders):
            for r in range(2):
                place = ((owner * orders + order) * 2 + r) * orders
                out_rows[place : place + orders, :] = value[
                    owner * orders : (owner + 1) * orders, r * width : (r + 1) * width
                ]
    out_ref[...] = out_rows[...].astype(jnp.bfloat16)


def analyse(legendre, rows):
    orders, degrees, _ = legendre.shape
    shape = (2 * orders * degrees, rows.shape[1])
    return pl.pallas_call(
        analyse_kernel,
        out_shape=jax.ShapeDtypeStruct(shape, jnp.bfloat16),
        in_specs=[VMEM] * 2,
        out_specs=VMEM,
        scratch_shapes=[pltpu.VMEM(rows.shape, jnp.float32), pltpu.VMEM(shape, jnp.float32)],
        compiler_params=limits(),
    )(legendre, rows)


def synthesise_kernel(order_ref, legendre_ref, scale_ref, in_ref, out_ref, in_rows, held, out_rows):
    orders, degrees, count_lat = legendre_ref.shape
    width = in_ref.shape[1]
    in_rows[...] = in_ref[...].astype(jnp.float32)
    degree = lax.broadcasted_iota(jnp.int32, held.shape, 0)
    for order in range(orders):
        for owner in range(degrees // orders):
            for r in range(2):
                place = ((owner * orders + order) * 2 + r) * orders
                held[owner * orders : (owner + 1) * orders, r * width : (r + 1) * width] = in_rows[
                    place : place + orders, :
                ]
        piece = jnp.where(degree >= order_ref[order], held[...], 0.0).astype(jnp.bfloat16)
        value = lax.dot_general(
            legendre_ref[order],
            piece,
            (((0,), (0,)), ((), ())),
            preferred_element_type=jnp.float32,
        )
        value = value * scale_ref[...]
        for r in range(2):
            out_rows[pl.ds(2 * order + r, count_lat, stride=2 * orders), :] = value[
                :, r * width : (r + 1) * width
            ]
    out_ref[...] = out_rows[...].astype(jnp.bfloat16)


def synthesise(order_ids, legendre, scale, rows):
    orders, degrees, count_lat = legendre.shape
    shape = (2 * orders * count_lat, rows.shape[1])
    return pl.pallas_call(
        synthesise_kernel,
        out_shape=jax.ShapeDtypeStruct(shape, jnp.bfloat16),
        in_specs=[SMEM] + [VMEM] * 3,
        out_specs=VMEM,
        scratch_shapes=[
            pltpu.VMEM(rows.shape, jnp.float32),
            pltpu.VMEM((degrees, 2 * rows.shape[1]), jnp.float32),
            pltpu.VMEM(shape, jnp.float32),
        ],
        compiler_params=limits(),
    )(order_ids, legendre, scale, rows)


def degree_rows(ref, degree, degrees, part):
    depth = 2 * degrees
    return pl.ds(part * degrees + degree, ref.shape[0] // depth, stride=depth)


def mix_kernel(adjoint_ref, mixing_ref, out_ref, in_rows, out_rows):
    degrees, width = mixing_ref.shape[:2]
    for owner in range(adjoint_ref.shape[0]):
        in_rows[...] = adjoint_ref[owner].astype(jnp.float32)
        for degree in range(degrees):
            places = [degree_rows(in_rows, degree, degrees, r) for r in range(2)]
            own = jnp.concatenate([in_rows[place, :] for place in places], axis=0)
            value = lax.dot_general(
                own.astype(jnp.bfloat16),
                mixing_ref[degree, :, owner * width : (owner + 1) * width],
                (((1,), (1,)), ((), ())),
                preferred_element_type=jnp.float32,
            )
            for r, place in enumerate(places):
                half = value[r * place.size : (r + 1) * place.size]
                out_rows[place, :] = half if owner == 0 else out_rows[place, :] + half
    out_ref[...] = out_rows[...].astype(jnp.bfloat16)


def mix(adjoint, mixing):
    return pl.pallas_call(
        mix_kernel,
        out_shape=jax.ShapeDtypeStruct(adjoint.shape[1:], jnp.bfloat16),
        in_specs=[VMEM] * 2,
        out_specs=VMEM,
        scratch_shapes=[pltpu.VMEM(adjoint.shape[1:], jnp.float32)] * 2,
        compiler_params=limits(),
    )(adjoint, mixing)


def weight_kernel(first_ref, order_ref, adjoint_ref, coefficient_ref, out_ref, other_rows, own_rows):
    degrees, width = out_ref.shape[:2]
    own_rows[...] = coefficient_ref[...].astype(jnp.float32)

    def read(rows, degree):
        kept = order_ref[...] <= first_ref[0] + degree
        pieces = [
            jnp.where(kept, rows[degree_rows(rows, degree, degrees, r), :], 0.0) for r in range(2)
        ]
        return jnp.concatenate(pieces, axis=0).astype(jnp.bfloat16)

    for owner in range(adjoint_ref.shape[0]):
        other_rows[...] = adjoint_ref[owner].astype(jnp.float32)
        for degree in range(degrees):
            out_ref[degree, :, owner * width : (owner + 1) * width] = lax.dot_general(
                read(own_rows, degree),
                read(other_rows, degree),
                (((0,), (0,)), ((), ())),
                preferred_element_type=jnp.float32,
            )


def weight_gradient(first, order_ids, adjoint, coefficients, degrees):
    lon_count, _, width = adjoint.shape
    order_rows = jnp.broadcast_to(order_ids[:, None], (order_ids.shape[0], width))
    return pl.pallas_call(
        weight_kernel,
        out_shape=jax.ShapeDtypeStruct((degrees, width, lon_count * width), jnp.float32),
        in_specs=[SMEM] + [VMEM] * 3,
        out_specs=VMEM,
        scratch_shapes=[pltpu.VMEM(coefficients.shape, jnp.float32)] * 2,
        compiler_params=limits(),
    )(first[None], order_rows, adjoint, coefficients)


def grid_kernel(table_ref, back_ref, field_ref, out_ref):
    lon_count, lat_count, height, width = back_ref.shape
    depth = height // PAIR
    back = back_ref[...].astype(jnp.float32)
    for row in range(PAIR):
        piece = [
            back[o, :, row * depth : (row + 1) * depth, :].reshape(lat_count * depth, width)
            for o in range(lon_count)
        ]
        full = jnp.concatenate(piece, axis=1).astype(jnp.bfloat16)
        value = jnp.dot(table_ref[...], full, preferred_element_type=jnp.float32)
        value = value.astype(jnp.bfloat16).astype(jnp.float32)
        out_ref[row] = (field_ref[row].astype(jnp.float32) + value).astype(jnp.bfloat16)


def grid_gradient(table, back, field):
    rows, points, channels = field.shape
    lon_count, lat_count, height, width = back.shape
    block = (PAIR, points, channels)
    return pl.pallas_call(
        grid_kernel,
        grid=(rows // PAIR,),
        out_shape=jax.ShapeDtypeStruct(field.shape, jnp.bfloat16),
        in_specs=[
            pl.BlockSpec(table.shape, lambda i: (0, 0)),
            pl.BlockSpec(
                (lon_count, lat_count, height // (rows // PAIR), width), lambda i: (0, 0, i, 0)
            ),
            pl.BlockSpec(block, lambda i: (i, 0, 0)),
        ],
        out_specs=pl.BlockSpec(block, lambda i: (i, 0, 0)),
        compiler_params=limits(),
    )(table, back, field)


def local(grid_input, cotangent, mixing):
    lat_count = lax.axis_size("lat")
    lon_count = lax.axis_size("lon")
    lat_rows, lon_rows, channels = grid_input.shape
    count_lat = lat_rows * lat_count
    count_lon = lon_rows * lon_count
    per_dev = mixing.shape[0]
    order_total = per_dev * lat_count
    block_ch = channels // lon_count
    lat_pos = lax.axis_index("lat")
    lon_pos = lax.axis_index("lon")
    slot_ids = jnp.arange(order_total, dtype=jnp.int32)
    slot_ids = slot_ids // per_dev + lat_count * (slot_ids % per_dev)
    forward, forward_rows, backward_rows = fourier_tables(
        slot_ids, lon_pos * lon_rows, lon_rows, count_lon
    )
    weights = quadrature(count_lat)
    own_weights = lax.dynamic_slice_in_dim(weights, lat_pos * lat_rows, lat_rows)
    own_orders = lat_pos + lat_count * jnp.arange(per_dev, dtype=jnp.int32)
    legendre = legendre_table(own_orders, count_lat, order_total, order_total)
    scale = weights[:, None]
    by_lat = (lat_count, -1, block_ch)
    by_both = (lon_count, -1, block_ch)
    flat = (-1, block_ch)

    part_g = partial_spectrum(
        cotangent, backward_rows, jnp.ones_like(own_weights), lat_count, lon_count
    )
    (rows_g,) = exchange(0, per_dev, (Reduce, None, part_g))
    part_x = partial_spectrum(grid_input, forward_rows, own_weights, lat_count, lon_count)
    adjoint = analyse(legendre, rows_g.reshape(flat))
    adjoint, rows_x = exchange(
        1, per_dev, (Spread, "out", adjoint.reshape(by_lat)), (Reduce, None, part_x)
    )
    adjoint = adjoint.reshape(by_both)
    mixed = mix(adjoint, mixing)
    (mixed,) = exchange(2, per_dev, (Swap, "home", mixed.reshape(by_lat)))
    back = synthesise(own_orders, legendre, scale, mixed.reshape(flat))
    coefficients = analyse(legendre, rows_x.reshape(flat))
    back, coefficients = exchange(
        3,
        per_dev,
        (Spread, None, back.reshape(by_lat)),
        (Swap, "out", coefficients.reshape(by_lat)),
    )
    input_grad = grid_gradient(forward, back, cotangent)
    weight_grad = weight_gradient(
        lat_pos * per_dev, slot_ids, adjoint, coefficients.reshape(flat), per_dev
    )
    return (input_grad, weight_grad)


def solution(mesh):
    in_specs = (P("lat", "lon", None), P("lat", "lon", None), P("lat", "lon", None))
    out_specs = (P("lat", "lon", None), P("lat", "lon", None))
    return jax.shard_map(local, mesh=mesh, in_specs=in_specs, out_specs=out_specs, check_vma=False)
```

```python
import functools
import math

import jax
import jax.numpy as jnp
from jax import lax
from jax.experimental import pallas as pl
from jax.experimental.pallas import tpu as pltpu
from jax.sharding import PartitionSpec as P


def quadrature(count_lat):
    colatitude = (jnp.arange(count_lat, dtype=jnp.float32) + 0.5) * (math.pi / count_lat)
    return math.pi / count_lat * jnp.sin(colatitude)


BLOCK = 16


def legendre_kernel(order_ref, cosine_ref, start_ref, out_ref, rows_ref):
    order = order_ref[...]
    cosine = cosine_ref[...]
    first_scale = jnp.sqrt(2.0 * order + 3.0)

    def advance(degree, carried):
        previous, earlier, scale_log = carried
        growth = jnp.sqrt(
            (4.0 * degree * degree - 1.0) / jnp.maximum(degree * degree - order * order, 1.0)
        )
        below = (degree - 1.0) * (degree - 1.0)
        shrink = jnp.sqrt(
            jnp.maximum(below - order * order, 0.0) / jnp.maximum(4.0 * below - 1.0, 1.0)
        )
        growth = jnp.where(degree == order + 1.0, first_scale, growth)
        growth = jnp.where(degree > order, growth, 0.0)
        current = growth * (cosine * previous - shrink * earlier)
        current = jnp.where(degree == order, 1.0, current)
        oversized = jnp.abs(current) > 10000000000.0
        factor = jnp.where(oversized, 1e-10, 1.0)
        scale_log = scale_log + jnp.where(oversized, math.log(10000000000.0), 0.0)
        current = current * factor
        return (current, previous * factor, scale_log), current * jnp.exp(scale_log)

    def block(index, carried):
        base = index * BLOCK
        for step in range(BLOCK):
            degree = (base + step).astype(jnp.float32)
            carried, value = advance(degree, carried)
            rows_ref[:, step, :] = value
        out_ref[:, pl.ds(pl.multiple_of(base, BLOCK), BLOCK), :] = rows_ref[...].astype(
            jnp.bfloat16
        )
        return carried

    zero = jnp.zeros(start_ref.shape, jnp.float32)
    lax.fori_loop(0, out_ref.shape[1] // BLOCK, block, (zero, zero, start_ref[...]))


def legendre_table(order_ids, count_lat, degrees, order_cap):
    colatitude = (jnp.arange(count_lat, dtype=jnp.float32) + 0.5) * (math.pi / count_lat)
    cosine = jnp.cos(colatitude)[None, :]
    sine_row = jnp.sin(colatitude)[None, :]
    order_value = order_ids.astype(jnp.float32)[:, None]
    counter = jnp.arange(1, order_cap + 1, dtype=jnp.float32)[None, :]
    log_terms = jnp.where(counter <= order_value, jnp.log1p(0.5 / counter), 0.0)
    log_start = (
        0.5 * math.log(0.5)
        + 0.5 * jnp.sum(log_terms, axis=1, keepdims=True)
        + order_value * jnp.log(sine_row)
    )
    orders = order_ids.shape[0]
    return pl.pallas_call(
        legendre_kernel,
        out_shape=jax.ShapeDtypeStruct((orders, degrees, count_lat), jnp.bfloat16),
        in_specs=[pl.BlockSpec(memory_space=pltpu.VMEM)] * 3,
        out_specs=pl.BlockSpec(memory_space=pltpu.VMEM),
        scratch_shapes=[pltpu.VMEM((orders, BLOCK, count_lat), jnp.float32)],
        compiler_params=pltpu.CompilerParams(vmem_limit_bytes=48 * 1024 * 1024),
    )(order_value, cosine, log_start)


def fourier_tables(order_ids, first, points_held, count_lon):
    points = first + jnp.arange(points_held, dtype=jnp.int32)
    phase_index = points[:, None] * order_ids[None, :] % count_lon
    angles = phase_index.astype(jnp.float32) * (2.0 * math.pi / count_lon)
    forward = jnp.stack([jnp.cos(angles), -jnp.sin(angles)], axis=2).reshape(
        points_held, 2 * order_ids.shape[0]
    )
    factor = jnp.where(order_ids == 0, 1.0, 2.0).astype(jnp.float32) / count_lon
    backward = forward * jnp.repeat(factor, 2)[None, :]
    return (forward.astype(jnp.bfloat16), backward.astype(jnp.bfloat16))


MESH = pl.DeviceIdType.MESH
VMEM = pl.BlockSpec(memory_space=pltpu.VMEM)
SMEM = pl.BlockSpec(memory_space=pltpu.SMEM)
ANY = pl.BlockSpec(memory_space=pl.ANY)


def limits(**more):
    return pltpu.CompilerParams(vmem_limit_bytes=48 * 1024 * 1024, **more)


def peer(axis, count, offset):
    return lax.rem(lax.axis_index(axis) + offset + count, count)


class Swap:
    def __init__(self, counts, source, target, landing, own_sem, sems):
        self.counts, self.source, self.target = counts, source, target
        self.landing, self.sems = landing, sems
        self.here = lax.axis_index("lat")
        self.own = pltpu.make_async_copy(
            source.at[self.here], landing.at[self.here], own_sem
        )

    def copy(self, offset):
        there = peer("lat", self.counts["lat"], offset)
        return pltpu.make_async_remote_copy(
            src_ref=self.source.at[there],
            dst_ref=self.landing.at[self.here],
            send_sem=self.sems.at[0, offset],
            recv_sem=self.sems.at[1, offset],
            device_id={"lat": there},
            device_id_type=MESH,
        )

    def each(self, act):
        def body(offset, carried):
            act(self.copy(offset))
            return carried

        lax.fori_loop(1, self.counts["lat"], body, 0)

    def start(self):
        self.each(lambda copy: copy.start())
        self.own.start()

    def first(self):
        pass

    def step(self, offset):
        pass

    def finish(self):
        self.own.wait()
        self.each(lambda copy: copy.wait())


class Later(Swap):
    def start(self):
        self.own.start()

    def step(self, offset):
        self.copy(offset).start()


class Spread(Swap):
    def __init__(self, counts, source, target, own_sem, sems, further):
        super().__init__(
            counts, source, target, target.at[lax.axis_index("lon")], own_sem, sems
        )
        self.further = further

    def onward(self, offset, ahead):
        slot = peer("lat", self.counts["lat"], -offset)
        return pltpu.make_async_remote_copy(
            src_ref=self.landing.at[slot],
            dst_ref=self.landing.at[slot],
            send_sem=self.further.at[0, ahead, offset],
            recv_sem=self.further.at[1, ahead, offset],
            device_id={"lon": peer("lon", self.counts["lon"], ahead)},
            device_id_type=MESH,
        )

    def first(self):
        self.own.wait()
        for ahead in range(1, self.counts["lon"]):
            self.onward(0, ahead).start()

    def step(self, offset):
        self.copy(offset).wait_recv()
        for ahead in range(1, self.counts["lon"]):
            self.onward(offset, ahead).start()

    def finish(self):
        self.each(lambda copy: copy.wait_send())

        def body(offset, carried):
            for ahead in range(1, self.counts["lon"]):
                self.onward(offset, ahead).wait()
            return carried

        lax.fori_loop(0, self.counts["lat"], body, 0)


class Reduce(Swap):
    def __init__(self, counts, source, target, own_sem, sems, further, sums, arrived, load_sem):
        super().__init__(counts, sums, target, target, own_sem, sems)
        self.parts, self.further, self.sums, self.arrived = source, further, sums, arrived
        self.load = pltpu.make_async_copy(source.at[lax.axis_index("lon")], sums, load_sem)

    def across(self, offset, ahead):
        slot = peer("lat", self.counts["lat"], offset)
        there = peer("lon", self.counts["lon"], ahead)
        return pltpu.make_async_remote_copy(
            src_ref=self.parts.at[there, slot],
            dst_ref=self.arrived.at[ahead - 1, slot],
            send_sem=self.further.at[0, ahead, offset],
            recv_sem=self.further.at[1, ahead, offset],
            device_id={"lon": there},
            device_id_type=MESH,
        )

    def every(self, begin, act):
        def body(offset, carried):
            for ahead in range(1, self.counts["lon"]):
                act(self.across(offset, ahead))
            return carried

        lax.fori_loop(begin, self.counts["lat"], body, 0)

    def start(self):
        self.load.start()
        self.every(1, lambda copy: copy.start())
        for ahead in range(1, self.counts["lon"]):
            self.across(0, ahead).start()

    def first(self):
        self.load.wait()

    def add(self, offset):
        slot = peer("lat", self.counts["lat"], offset)
        total = self.sums[slot].astype(jnp.float32)
        for ahead in range(1, self.counts["lon"]):
            self.across(offset, ahead).wait_recv()
            total = total + self.arrived[ahead - 1, slot].astype(jnp.float32)
        self.sums[slot] = total.astype(jnp.bfloat16)

    def step(self, offset):
        self.add(offset)
        self.copy(offset).start()

    def finish(self):
        self.add(0)
        self.own.start()
        self.own.wait()
        self.each(lambda copy: copy.wait())
        self.every(0, lambda copy: copy.wait_send())


def exchange_kernel(kinds, counts, lengths, *refs):
    total = len(kinds)
    sources, targets, scratch = refs[:total], refs[total : 2 * total], refs[2 * total :]

    barrier = pltpu.get_barrier_semaphore()
    expected = 0
    for axis in ("lon", "lat") if set(kinds) != {Swap} else ("lat",):

        def greet(offset, carried, axis=axis):
            there = peer(axis, counts[axis], offset)
            pl.semaphore_signal(barrier, inc=1, device_id={axis: there}, device_id_type=MESH)
            return carried

        lax.fori_loop(1, counts[axis], greet, 0)
        expected += counts[axis] - 1
    pl.semaphore_wait(barrier, expected)

    jobs, place = [], 0
    for kind, length, source, target in zip(kinds, lengths, sources, targets):
        held = scratch[place : place + length]
        landing = (target,) if kind in (Swap, Later) else ()
        jobs.append(kind(counts, source, target, *landing, *held))
        place += length
    for job in jobs:
        job.start()
    for job in jobs:
        job.first()

    if set(kinds) != {Swap}:

        def body(offset, carried):
            for job in jobs:
                job.step(offset)
            return carried

        lax.fori_loop(1, counts["lat"], body, 0)
    for job in jobs:
        job.finish()


def exchange(ident, *pairs):
    counts = {"lat": lax.axis_size("lat"), "lon": lax.axis_size("lon")}
    kinds = [kind for kind, _ in pairs]
    arrays = [array for _, array in pairs]
    dma = pltpu.SemaphoreType.DMA
    shapes, scratch, lengths = [], [], []
    for kind, array in pairs:
        shape = array.shape
        held = [dma, dma((2, counts["lat"]))]
        if kind in (Spread, Reduce):
            held.append(dma((2, counts["lon"], counts["lat"])))
        if kind is Spread:
            shape = (counts["lon"],) + shape
        if kind is Reduce:
            shape = shape[1:]
            held.append(pltpu.VMEM(shape, array.dtype))
            held.append(pltpu.VMEM((counts["lon"] - 1,) + shape, array.dtype))
            held.append(dma)
        shapes.append(jax.ShapeDtypeStruct(shape, array.dtype))
        scratch += held
        lengths.append(len(held))
    return pl.pallas_call(
        functools.partial(exchange_kernel, kinds, counts, lengths),
        out_shape=shapes,
        in_specs=[ANY] * len(arrays),
        out_specs=[ANY] * len(arrays),
        scratch_shapes=scratch,
        compiler_params=limits(collective_id=ident, has_side_effects=True),
    )(*arrays)


PAIR = 2


def spectrum_kernel(lon_count, scale_ref, table_ref, field_ref, out_ref):
    _, lat_count, depth, width = out_ref.shape
    step = pl.program_id(0)
    parts = []
    for row in range(PAIR):
        part = jnp.dot(table_ref[...], field_ref[row], preferred_element_type=jnp.float32)
        parts.append(part * scale_ref[step * PAIR + row])
    for owner in range(lon_count):
        piece = [
            part[:, owner * width : (owner + 1) * width].reshape(lat_count, depth // PAIR, width)
            for part in parts
        ]
        out_ref[owner] = jnp.concatenate(piece, axis=1).astype(jnp.bfloat16)


def partial_spectrum(field, table, scale, lat_count, lon_count, begin=0, end=None):
    _, points, channels = field.shape
    end = field.shape[0] if end is None else end
    rows = end - begin
    orders = table.shape[0] // lat_count
    width = channels // lon_count
    block = (lon_count, lat_count, PAIR * orders, width)
    return pl.pallas_call(
        functools.partial(spectrum_kernel, lon_count),
        grid=(rows // PAIR,),
        out_shape=jax.ShapeDtypeStruct(
            (lon_count, lat_count, rows * orders, width), jnp.bfloat16
        ),
        in_specs=[
            SMEM,
            pl.BlockSpec(table.shape, lambda i: (0, 0)),
            pl.BlockSpec((PAIR, points, channels), lambda i: (i + begin // PAIR, 0, 0)),
        ],
        out_specs=pl.BlockSpec(block, lambda i: (0, 0, i, 0)),
        compiler_params=limits(),
    )(scale[begin:end], table, field)


def transform_kernel(forward, legendre_ref, scale_ref, in_ref, out_ref, in_rows, out_rows):
    orders, degrees, count_lat = legendre_ref.shape
    taken, given = (count_lat, degrees) if forward else (degrees, count_lat)
    width = in_ref.shape[1]
    in_rows[...] = in_ref[...].astype(jnp.float32)
    for order in range(orders):
        piece = [in_rows[pl.ds(2 * order + r, taken, stride=2 * orders), :] for r in range(2)]
        value = lax.dot_general(
            legendre_ref[order],
            jnp.concatenate(piece, axis=1).astype(jnp.bfloat16),
            (((1 if forward else 0,), (0,)), ((), ())),
            preferred_element_type=jnp.float32,
        )
        if not forward:
            value = value * scale_ref[...]
        for r in range(2):
            out_rows[pl.ds(2 * order + r, given, stride=2 * orders), :] = value[
                :, r * width : (r + 1) * width
            ]
    out_ref[...] = out_rows[...].astype(jnp.bfloat16)


def transform(forward, legendre, scale, rows):
    orders, degrees, count_lat = legendre.shape
    height = 2 * orders * (degrees if forward else count_lat)
    return pl.pallas_call(
        functools.partial(transform_kernel, forward),
        out_shape=jax.ShapeDtypeStruct((height, rows.shape[1]), jnp.bfloat16),
        in_specs=[VMEM] * 3,
        out_specs=VMEM,
        scratch_shapes=[
            pltpu.VMEM(rows.shape, jnp.float32),
            pltpu.VMEM((height, rows.shape[1]), jnp.float32),
        ],
        compiler_params=limits(),
    )(legendre, scale, rows)


def degree_rows(ref, lead, pair, depth):
    block = ref[lead + (slice(None), slice(pair * PAIR * depth, (pair + 1) * PAIR * depth))]
    block = block.astype(jnp.float32)
    count, _, width = block.shape
    return [
        block[:, i * depth : (i + 1) * depth].reshape(count * depth, width).astype(jnp.bfloat16)
        for i in range(PAIR)
    ]


def all_channels(ref, pair, depth):
    owners = [degree_rows(ref, (o,), pair, depth) for o in range(ref.shape[0])]
    return [jnp.concatenate([rows[i] for rows in owners], axis=1) for i in range(PAIR)]


def mix_kernel(adjoint_ref, mixing_ref, out_ref):
    degrees, width = mixing_ref.shape[:2]
    _, lat_count, height, _ = adjoint_ref.shape
    depth = height // degrees
    for pair in range(degrees // PAIR):
        values = []
        for i, full in enumerate(all_channels(adjoint_ref, pair, depth)):
            value = lax.dot_general(
                full,
                mixing_ref[pair * PAIR + i],
                (((1,), (1,)), ((), ())),
                preferred_element_type=jnp.float32,
            )
            values.append(value.reshape(lat_count, depth, width))
        out_ref[:, pair * PAIR * depth : (pair + 1) * PAIR * depth, :] = jnp.concatenate(
            values, axis=1
        ).astype(jnp.bfloat16)


def mix(adjoint, mixing):
    return pl.pallas_call(
        mix_kernel,
        out_shape=jax.ShapeDtypeStruct(adjoint.shape[1:], jnp.bfloat16),
        in_specs=[VMEM] * 2,
        out_specs=VMEM,
        compiler_params=limits(),
    )(adjoint, mixing)


def weight_kernel(adjoint_ref, coefficient_ref, out_ref):
    degrees = out_ref.shape[0]
    depth = adjoint_ref.shape[2] // degrees
    for pair in range(degrees // PAIR):
        full = all_channels(adjoint_ref, pair, depth)
        own = degree_rows(coefficient_ref, (), pair, depth)
        for i in range(PAIR):
            out_ref[pair * PAIR + i] = lax.dot_general(
                own[i], full[i], (((0,), (0,)), ((), ())), preferred_element_type=jnp.float32
            )


def weight_gradient(adjoint, coefficients, degrees):
    lon_count, _, _, width = adjoint.shape
    return pl.pallas_call(
        weight_kernel,
        out_shape=jax.ShapeDtypeStruct((degrees, width, lon_count * width), jnp.float32),
        in_specs=[VMEM] * 2,
        out_specs=VMEM,
        compiler_params=limits(),
    )(adjoint, coefficients)


def grid_kernel(table_ref, back_ref, field_ref, out_ref):
    lon_count, lat_count, height, width = back_ref.shape
    depth = height // PAIR
    back = back_ref[...].astype(jnp.float32)
    for row in range(PAIR):
        piece = [
            back[o, :, row * depth : (row + 1) * depth, :].reshape(lat_count * depth, width)
            for o in range(lon_count)
        ]
        full = jnp.concatenate(piece, axis=1).astype(jnp.bfloat16)
        value = jnp.dot(table_ref[...], full, preferred_element_type=jnp.float32)
        value = value.astype(jnp.bfloat16).astype(jnp.float32)
        out_ref[row] = (field_ref[row].astype(jnp.float32) + value).astype(jnp.bfloat16)


def grid_gradient(table, back, field):
    rows, points, channels = field.shape
    lon_count, lat_count, height, width = back.shape
    block = (PAIR, points, channels)
    return pl.pallas_call(
        grid_kernel,
        grid=(rows // PAIR,),
        out_shape=jax.ShapeDtypeStruct(field.shape, jnp.bfloat16),
        in_specs=[
            pl.BlockSpec(table.shape, lambda i: (0, 0)),
            pl.BlockSpec(
                (lon_count, lat_count, height // (rows // PAIR), width), lambda i: (0, 0, i, 0)
            ),
            pl.BlockSpec(block, lambda i: (i, 0, 0)),
        ],
        out_specs=pl.BlockSpec(block, lambda i: (i, 0, 0)),
        compiler_params=limits(),
    )(table, back, field)


def local(grid_input, cotangent, mixing):
    lat_count = lax.axis_size("lat")
    lon_count = lax.axis_size("lon")
    lat_rows, lon_rows, channels = grid_input.shape
    count_lat = lat_rows * lat_count
    count_lon = lon_rows * lon_count
    per_dev = mixing.shape[0]
    order_total = per_dev * lat_count
    block_ch = channels // lon_count
    lat_pos = lax.axis_index("lat")
    lon_pos = lax.axis_index("lon")
    slot_ids = jnp.arange(order_total, dtype=jnp.int32)
    forward, backward = fourier_tables(slot_ids, lon_pos * lon_rows, lon_rows, count_lon)
    weights = quadrature(count_lat)
    own_weights = lax.dynamic_slice_in_dim(weights, lat_pos * lat_rows, lat_rows)
    own_orders = lat_pos * per_dev + jnp.arange(per_dev, dtype=jnp.int32)
    legendre = legendre_table(own_orders, count_lat, order_total, order_total)
    scale = weights[:, None]
    by_lat = (lat_count, -1, block_ch)
    flat = (-1, block_ch)

    part_g = partial_spectrum(
        cotangent, backward.T, jnp.ones_like(own_weights), lat_count, lon_count
    )
    (rows_g,) = exchange(0, (Reduce, part_g))
    middle = lat_rows // PAIR // 2 * PAIR
    parts_x = [
        partial_spectrum(grid_input, forward.T, own_weights, lat_count, lon_count, *rows)
        for rows in ((0, middle), (middle, lat_rows))
    ]
    adjoint = transform(True, legendre, scale, rows_g.reshape(flat))
    adjoint, upper_x = exchange(1, (Spread, adjoint.reshape(by_lat)), (Reduce, parts_x[0]))
    mixed, lower_x = exchange(2, (Swap, mix(adjoint, mixing)), (Reduce, parts_x[1]))
    rows_x = jnp.concatenate([upper_x, lower_x], axis=1)
    back = transform(False, legendre, scale, mixed.reshape(flat))
    coefficients = transform(True, legendre, scale, rows_x.reshape(flat))
    back, coefficients = exchange(
        3, (Spread, back.reshape(by_lat)), (Later, coefficients.reshape(by_lat))
    )
    input_grad = grid_gradient(forward, back, cotangent)
    weight_grad = weight_gradient(adjoint, coefficients, per_dev)
    return (input_grad, weight_grad)


def solution(mesh):
    in_specs = (P("lat", "lon", None), P("lat", "lon", None), P("lat", "lon", None))
    out_specs = (P("lat", "lon", None), P("lat", "lon", None))
    return jax.shard_map(local, mesh=mesh, in_specs=in_specs, out_specs=out_specs, check_vma=False)
```

```python
import functools
import math

import jax
import jax.numpy as jnp
from jax import lax
from jax.experimental import pallas as pl
from jax.experimental.pallas import tpu as pltpu
from jax.sharding import PartitionSpec as P


def quadrature(count_lat):
    colatitude = (jnp.arange(count_lat, dtype=jnp.float32) + 0.5) * (math.pi / count_lat)
    return math.pi / count_lat * jnp.sin(colatitude)


BLOCK = 16


def legendre_kernel(order_ref, cosine_ref, start_ref, out_ref, rows_ref):
    order = order_ref[...]
    cosine = cosine_ref[...]
    first_scale = jnp.sqrt(2.0 * order + 3.0)

    def advance(degree, carried):
        previous, earlier, scale_log = carried
        growth = jnp.sqrt(
            (4.0 * degree * degree - 1.0) / jnp.maximum(degree * degree - order * order, 1.0)
        )
        below = (degree - 1.0) * (degree - 1.0)
        shrink = jnp.sqrt(
            jnp.maximum(below - order * order, 0.0) / jnp.maximum(4.0 * below - 1.0, 1.0)
        )
        growth = jnp.where(degree == order + 1.0, first_scale, growth)
        growth = jnp.where(degree > order, growth, 0.0)
        current = growth * (cosine * previous - shrink * earlier)
        current = jnp.where(degree == order, 1.0, current)
        oversized = jnp.abs(current) > 10000000000.0
        factor = jnp.where(oversized, 1e-10, 1.0)
        scale_log = scale_log + jnp.where(oversized, math.log(10000000000.0), 0.0)
        current = current * factor
        return (current, previous * factor, scale_log), current * jnp.exp(scale_log)

    def block(index, carried):
        base = index * BLOCK
        for step in range(BLOCK):
            degree = (base + step).astype(jnp.float32)
            carried, value = advance(degree, carried)
            rows_ref[:, step, :] = value
        out_ref[:, pl.ds(pl.multiple_of(base, BLOCK), BLOCK), :] = rows_ref[...].astype(
            jnp.bfloat16
        )
        return carried

    zero = jnp.zeros(start_ref.shape, jnp.float32)
    lax.fori_loop(0, out_ref.shape[1] // BLOCK, block, (zero, zero, start_ref[...]))


def legendre_table(order_ids, count_lat, degrees, order_cap):
    colatitude = (jnp.arange(count_lat, dtype=jnp.float32) + 0.5) * (math.pi / count_lat)
    cosine = jnp.cos(colatitude)[None, :]
    sine_row = jnp.sin(colatitude)[None, :]
    order_value = order_ids.astype(jnp.float32)[:, None]
    counter = jnp.arange(1, order_cap + 1, dtype=jnp.float32)[None, :]
    log_terms = jnp.where(counter <= order_value, jnp.log1p(0.5 / counter), 0.0)
    log_start = (
        0.5 * math.log(0.5)
        + 0.5 * jnp.sum(log_terms, axis=1, keepdims=True)
        + order_value * jnp.log(sine_row)
    )
    orders = order_ids.shape[0]
    return pl.pallas_call(
        legendre_kernel,
        out_shape=jax.ShapeDtypeStruct((orders, degrees, count_lat), jnp.bfloat16),
        in_specs=[pl.BlockSpec(memory_space=pltpu.VMEM)] * 3,
        out_specs=pl.BlockSpec(memory_space=pltpu.VMEM),
        scratch_shapes=[pltpu.VMEM((orders, BLOCK, count_lat), jnp.float32)],
        compiler_params=pltpu.CompilerParams(vmem_limit_bytes=48 * 1024 * 1024),
    )(order_value, cosine, log_start)


def fourier_tables(order_ids, first, points_held, count_lon):
    points = first + jnp.arange(points_held, dtype=jnp.int32)
    phase_index = points[:, None] * order_ids[None, :] % count_lon
    angles = phase_index.astype(jnp.float32) * (2.0 * math.pi / count_lon)
    forward = jnp.stack([jnp.cos(angles), -jnp.sin(angles)], axis=2).reshape(
        points_held, 2 * order_ids.shape[0]
    )
    factor = jnp.where(order_ids == 0, 1.0, 2.0).astype(jnp.float32) / count_lon
    backward = forward * jnp.repeat(factor, 2)[None, :]
    return (forward.astype(jnp.bfloat16), backward.astype(jnp.bfloat16))


MESH = pl.DeviceIdType.MESH
WINDOW = 6
VMEM = pl.BlockSpec(memory_space=pltpu.VMEM)
SMEM = pl.BlockSpec(memory_space=pltpu.SMEM)
ANY = pl.BlockSpec(memory_space=pl.ANY)


def limits(**more):
    return pltpu.CompilerParams(vmem_limit_bytes=48 * 1024 * 1024, **more)


def peer(axis, count, offset):
    return lax.rem(lax.axis_index(axis) + offset + count, count)


class Swap:
    def __init__(self, counts, source, target, landing, own_sem, sems):
        self.counts, self.source, self.target = counts, source, target
        self.landing, self.sems = landing, sems
        self.here = lax.axis_index("lat")
        self.own = pltpu.make_async_copy(
            source.at[self.here], landing.at[self.here], own_sem
        )

    def copy(self, offset):
        there = peer("lat", self.counts["lat"], offset)
        return pltpu.make_async_remote_copy(
            src_ref=self.source.at[there],
            dst_ref=self.landing.at[self.here],
            send_sem=self.sems.at[0, offset],
            recv_sem=self.sems.at[1, offset],
            device_id={"lat": there},
            device_id_type=MESH,
        )

    def each(self, act):
        def body(offset, carried):
            act(self.copy(offset))
            return carried

        lax.fori_loop(1, self.counts["lat"], body, 0)

    def start(self):
        self.each(lambda copy: copy.start())
        self.own.start()

    def first(self):
        pass

    def step(self, offset):
        pass

    def finish(self):
        self.own.wait()
        self.each(lambda copy: copy.wait())


class Spread(Swap):
    def __init__(self, counts, source, target, own_sem, sems, further):
        super().__init__(
            counts, source, target, target.at[lax.axis_index("lon")], own_sem, sems
        )
        self.further = further

    def onward(self, offset, ahead):
        slot = peer("lat", self.counts["lat"], -offset)
        return pltpu.make_async_remote_copy(
            src_ref=self.landing.at[slot],
            dst_ref=self.landing.at[slot],
            send_sem=self.further.at[0, ahead, offset],
            recv_sem=self.further.at[1, ahead, offset],
            device_id={"lon": peer("lon", self.counts["lon"], ahead)},
            device_id_type=MESH,
        )

    def first(self):
        self.own.wait()
        for ahead in range(1, self.counts["lon"]):
            self.onward(0, ahead).start()

    def start(self):
        self.own.start()
        for offset in range(1, min(WINDOW + 1, self.counts["lat"])):
            self.copy(offset).start()

    def step(self, offset):
        self.copy(offset).wait_recv()
        for ahead in range(1, self.counts["lon"]):
            self.onward(offset, ahead).start()

        @pl.when(offset + WINDOW < self.counts["lat"])
        def _():
            self.copy(offset + WINDOW).start()

    def finish(self):
        self.each(lambda copy: copy.wait_send())

        def body(offset, carried):
            for ahead in range(1, self.counts["lon"]):
                self.onward(offset, ahead).wait()
            return carried

        lax.fori_loop(0, self.counts["lat"], body, 0)


class Reduce(Swap):
    def __init__(self, counts, source, target, own_sem, sems, further, sums, arrived, load_sem):
        super().__init__(counts, sums, target, target, own_sem, sems)
        self.parts, self.further, self.sums, self.arrived = source, further, sums, arrived
        self.load = pltpu.make_async_copy(source.at[lax.axis_index("lon")], sums, load_sem)

    def across(self, offset, ahead):
        slot = peer("lat", self.counts["lat"], offset)
        there = peer("lon", self.counts["lon"], ahead)
        return pltpu.make_async_remote_copy(
            src_ref=self.parts.at[there, slot],
            dst_ref=self.arrived.at[ahead - 1, slot],
            send_sem=self.further.at[0, ahead, offset],
            recv_sem=self.further.at[1, ahead, offset],
            device_id={"lon": there},
            device_id_type=MESH,
        )

    def every(self, begin, act):
        def body(offset, carried):
            for ahead in range(1, self.counts["lon"]):
                act(self.across(offset, ahead))
            return carried

        lax.fori_loop(begin, self.counts["lat"], body, 0)

    def start(self):
        self.load.start()
        self.every(1, lambda copy: copy.start())
        for ahead in range(1, self.counts["lon"]):
            self.across(0, ahead).start()

    def first(self):
        self.load.wait()

    def add(self, offset):
        slot = peer("lat", self.counts["lat"], offset)
        total = self.sums[slot].astype(jnp.float32)
        for ahead in range(1, self.counts["lon"]):
            self.across(offset, ahead).wait_recv()
            total = total + self.arrived[ahead - 1, slot].astype(jnp.float32)
        self.sums[slot] = total.astype(jnp.bfloat16)

    def step(self, offset):
        self.add(offset)
        self.copy(offset).start()

    def finish(self):
        self.add(0)
        self.own.start()
        self.own.wait()
        self.each(lambda copy: copy.wait())
        self.every(0, lambda copy: copy.wait_send())


def exchange_kernel(kinds, counts, lengths, *refs):
    total = len(kinds)
    sources, targets, scratch = refs[:total], refs[total : 2 * total], refs[2 * total :]

    barrier = pltpu.get_barrier_semaphore()
    expected = 0
    for axis in ("lon", "lat") if set(kinds) != {Swap} else ("lat",):

        def greet(offset, carried, axis=axis):
            there = peer(axis, counts[axis], offset)
            pl.semaphore_signal(barrier, inc=1, device_id={axis: there}, device_id_type=MESH)
            return carried

        lax.fori_loop(1, counts[axis], greet, 0)
        expected += counts[axis] - 1
    pl.semaphore_wait(barrier, expected)

    jobs, place = [], 0
    for kind, length, source, target in zip(kinds, lengths, sources, targets):
        held = scratch[place : place + length]
        landing = (target,) if kind is Swap else ()
        jobs.append(kind(counts, source, target, *landing, *held))
        place += length
    for job in jobs:
        job.start()
    for job in jobs:
        job.first()

    if set(kinds) != {Swap}:

        def body(offset, carried):
            for job in jobs:
                job.step(offset)
            return carried

        lax.fori_loop(1, counts["lat"], body, 0)
    for job in jobs:
        job.finish()


def exchange(ident, *pairs):
    counts = {"lat": lax.axis_size("lat"), "lon": lax.axis_size("lon")}
    kinds = [kind for kind, _ in pairs]
    arrays = [array for _, array in pairs]
    dma = pltpu.SemaphoreType.DMA
    shapes, scratch, lengths = [], [], []
    for kind, array in pairs:
        shape = array.shape
        held = [dma, dma((2, counts["lat"]))]
        if kind is not Swap:
            held.append(dma((2, counts["lon"], counts["lat"])))
        if kind is Spread:
            shape = (counts["lon"],) + shape
        if kind is Reduce:
            shape = shape[1:]
            held.append(pltpu.VMEM(shape, array.dtype))
            held.append(pltpu.VMEM((counts["lon"] - 1,) + shape, array.dtype))
            held.append(dma)
        shapes.append(jax.ShapeDtypeStruct(shape, array.dtype))
        scratch += held
        lengths.append(len(held))
    return pl.pallas_call(
        functools.partial(exchange_kernel, kinds, counts, lengths),
        out_shape=shapes,
        in_specs=[ANY] * len(arrays),
        out_specs=[ANY] * len(arrays),
        scratch_shapes=scratch,
        compiler_params=limits(collective_id=ident, has_side_effects=True),
    )(*arrays)


PAIR = 2


def spectrum_kernel(lon_count, scale_ref, table_ref, field_ref, out_ref):
    _, lat_count, depth, width = out_ref.shape
    step = pl.program_id(0)
    parts = []
    for row in range(PAIR):
        part = jnp.dot(table_ref[...], field_ref[row], preferred_element_type=jnp.float32)
        parts.append(part * scale_ref[step * PAIR + row])
    for owner in range(lon_count):
        piece = [
            part[:, owner * width : (owner + 1) * width].reshape(lat_count, depth // PAIR, width)
            for part in parts
        ]
        out_ref[owner] = jnp.concatenate(piece, axis=1).astype(jnp.bfloat16)


def partial_spectrum(field, table, scale, lat_count, lon_count):
    rows, points, channels = field.shape
    orders = table.shape[0] // lat_count
    width = channels // lon_count
    block = (lon_count, lat_count, PAIR * orders, width)
    return pl.pallas_call(
        functools.partial(spectrum_kernel, lon_count),
        grid=(rows // PAIR,),
        out_shape=jax.ShapeDtypeStruct(
            (lon_count, lat_count, rows * orders, width), jnp.bfloat16
        ),
        in_specs=[
            SMEM,
            pl.BlockSpec(table.shape, lambda i: (0, 0)),
            pl.BlockSpec((PAIR, points, channels), lambda i: (i, 0, 0)),
        ],
        out_specs=pl.BlockSpec(block, lambda i: (0, 0, i, 0)),
        compiler_params=limits(),
    )(scale, table, field)


def transform_kernel(forward, legendre_ref, scale_ref, in_ref, out_ref, in_rows, out_rows):
    orders, degrees, count_lat = legendre_ref.shape
    taken, given = (count_lat, degrees) if forward else (degrees, count_lat)
    width = in_ref.shape[1]
    in_rows[...] = in_ref[...].astype(jnp.float32)
    for order in range(orders):
        piece = [in_rows[pl.ds(2 * order + r, taken, stride=2 * orders), :] for r in range(2)]
        value = lax.dot_general(
            legendre_ref[order],
            jnp.concatenate(piece, axis=1).astype(jnp.bfloat16),
            (((1 if forward else 0,), (0,)), ((), ())),
            preferred_element_type=jnp.float32,
        )
        if not forward:
            value = value * scale_ref[...]
        for r in range(2):
            out_rows[pl.ds(2 * order + r, given, stride=2 * orders), :] = value[
                :, r * width : (r + 1) * width
            ]
    out_ref[...] = out_rows[...].astype(jnp.bfloat16)


def transform(forward, legendre, scale, rows):
    orders, degrees, count_lat = legendre.shape
    height = 2 * orders * (degrees if forward else count_lat)
    return pl.pallas_call(
        functools.partial(transform_kernel, forward),
        out_shape=jax.ShapeDtypeStruct((height, rows.shape[1]), jnp.bfloat16),
        in_specs=[VMEM] * 3,
        out_specs=VMEM,
        scratch_shapes=[
            pltpu.VMEM(rows.shape, jnp.float32),
            pltpu.VMEM((height, rows.shape[1]), jnp.float32),
        ],
        compiler_params=limits(),
    )(legendre, scale, rows)


def degree_rows(ref, lead, pair, depth):
    block = ref[lead + (slice(None), slice(pair * PAIR * depth, (pair + 1) * PAIR * depth))]
    block = block.astype(jnp.float32)
    count, _, width = block.shape
    return [
        block[:, i * depth : (i + 1) * depth].reshape(count * depth, width).astype(jnp.bfloat16)
        for i in range(PAIR)
    ]


def all_channels(ref, pair, depth):
    owners = [degree_rows(ref, (o,), pair, depth) for o in range(ref.shape[0])]
    return [jnp.concatenate([rows[i] for rows in owners], axis=1) for i in range(PAIR)]


def mix_kernel(adjoint_ref, mixing_ref, out_ref):
    degrees, width = mixing_ref.shape[:2]
    _, lat_count, height, _ = adjoint_ref.shape
    depth = height // degrees
    for pair in range(degrees // PAIR):
        values = []
        for i, full in enumerate(all_channels(adjoint_ref, pair, depth)):
            value = lax.dot_general(
                full,
                mixing_ref[pair * PAIR + i],
                (((1,), (1,)), ((), ())),
                preferred_element_type=jnp.float32,
            )
            values.append(value.reshape(lat_count, depth, width))
        out_ref[:, pair * PAIR * depth : (pair + 1) * PAIR * depth, :] = jnp.concatenate(
            values, axis=1
        ).astype(jnp.bfloat16)


def mix(adjoint, mixing):
    return pl.pallas_call(
        mix_kernel,
        out_shape=jax.ShapeDtypeStruct(adjoint.shape[1:], jnp.bfloat16),
        in_specs=[VMEM] * 2,
        out_specs=VMEM,
        compiler_params=limits(),
    )(adjoint, mixing)


def weight_kernel(adjoint_ref, coefficient_ref, out_ref):
    degrees = out_ref.shape[0]
    depth = adjoint_ref.shape[2] // degrees
    for pair in range(degrees // PAIR):
        full = all_channels(adjoint_ref, pair, depth)
        own = degree_rows(coefficient_ref, (), pair, depth)
        for i in range(PAIR):
            out_ref[pair * PAIR + i] = lax.dot_general(
                own[i], full[i], (((0,), (0,)), ((), ())), preferred_element_type=jnp.float32
            )


def weight_gradient(adjoint, coefficients, degrees):
    lon_count, _, _, width = adjoint.shape
    return pl.pallas_call(
        weight_kernel,
        out_shape=jax.ShapeDtypeStruct((degrees, width, lon_count * width), jnp.float32),
        in_specs=[VMEM] * 2,
        out_specs=VMEM,
        compiler_params=limits(),
    )(adjoint, coefficients)


def grid_kernel(table_ref, back_ref, field_ref, out_ref):
    lon_count, lat_count, height, width = back_ref.shape
    depth = height // PAIR
    back = back_ref[...].astype(jnp.float32)
    for row in range(PAIR):
        piece = [
            back[o, :, row * depth : (row + 1) * depth, :].reshape(lat_count * depth, width)
            for o in range(lon_count)
        ]
        full = jnp.concatenate(piece, axis=1).astype(jnp.bfloat16)
        value = jnp.dot(table_ref[...], full, preferred_element_type=jnp.float32)
        value = value.astype(jnp.bfloat16).astype(jnp.float32)
        out_ref[row] = (field_ref[row].astype(jnp.float32) + value).astype(jnp.bfloat16)


def grid_gradient(table, back, field):
    rows, points, channels = field.shape
    lon_count, lat_count, height, width = back.shape
    block = (PAIR, points, channels)
    return pl.pallas_call(
        grid_kernel,
        grid=(rows // PAIR,),
        out_shape=jax.ShapeDtypeStruct(field.shape, jnp.bfloat16),
        in_specs=[
            pl.BlockSpec(table.shape, lambda i: (0, 0)),
            pl.BlockSpec(
                (lon_count, lat_count, height // (rows // PAIR), width), lambda i: (0, 0, i, 0)
            ),
            pl.BlockSpec(block, lambda i: (i, 0, 0)),
        ],
        out_specs=pl.BlockSpec(block, lambda i: (i, 0, 0)),
        compiler_params=limits(),
    )(table, back, field)


def local(grid_input, cotangent, mixing):
    lat_count = lax.axis_size("lat")
    lon_count = lax.axis_size("lon")
    lat_rows, lon_rows, channels = grid_input.shape
    count_lat = lat_rows * lat_count
    count_lon = lon_rows * lon_count
    per_dev = mixing.shape[0]
    order_total = per_dev * lat_count
    block_ch = channels // lon_count
    lat_pos = lax.axis_index("lat")
    lon_pos = lax.axis_index("lon")
    slot_ids = jnp.arange(order_total, dtype=jnp.int32)
    forward, backward = fourier_tables(slot_ids, lon_pos * lon_rows, lon_rows, count_lon)
    weights = quadrature(count_lat)
    own_weights = lax.dynamic_slice_in_dim(weights, lat_pos * lat_rows, lat_rows)
    own_orders = lat_pos * per_dev + jnp.arange(per_dev, dtype=jnp.int32)
    legendre = legendre_table(own_orders, count_lat, order_total, order_total)
    scale = weights[:, None]
    by_lat = (lat_count, -1, block_ch)
    flat = (-1, block_ch)

    part_g = partial_spectrum(
        cotangent, backward.T, jnp.ones_like(own_weights), lat_count, lon_count
    )
    (rows_g,) = exchange(0, (Reduce, part_g))
    part_x = partial_spectrum(grid_input, forward.T, own_weights, lat_count, lon_count)
    adjoint = transform(True, legendre, scale, rows_g.reshape(flat))
    adjoint, rows_x = exchange(1, (Spread, adjoint.reshape(by_lat)), (Reduce, part_x))
    (mixed,) = exchange(2, (Swap, mix(adjoint, mixing)))
    back = transform(False, legendre, scale, mixed.reshape(flat))
    coefficients = transform(True, legendre, scale, rows_x.reshape(flat))
    back, coefficients = exchange(
        3, (Spread, back.reshape(by_lat)), (Swap, coefficients.reshape(by_lat))
    )
    input_grad = grid_gradient(forward, back, cotangent)
    weight_grad = weight_gradient(adjoint, coefficients, per_dev)
    return (input_grad, weight_grad)


def solution(mesh):
    in_specs = (P("lat", "lon", None), P("lat", "lon", None), P("lat", "lon", None))
    out_specs = (P("lat", "lon", None), P("lat", "lon", None))
    return jax.shard_map(local, mesh=mesh, in_specs=in_specs, out_specs=out_specs, check_vma=False)
```
